32 devices in a mesh: ctx: 8 (over z, core), expert: 4 (over y, x).
Axes of the slice: x: 2, y: 2, z: 4, core: 2. Of those that a mesh axis runs over, the one named last changes fastest.
Arguments:
- inputs: bfloat16 [4, 4096, 1536], P('expert', 'ctx'), may hold values from -6 to 6
- cotangent: bfloat16 [4, 4096, 1536], P('expert', 'ctx'), may hold values from -6 to 6
- routes: int32 [4, 4096, 8], P('expert', 'ctx'), may hold values from 0 to 39, all different within a row; in each aligned block of 512 rows (0 to 511, 512 to 1023, ..., all dimensions but the last counted through in order) at most 128 rows name the same one
- attn_gain: bfloat16 [1536], P('ctx'), may hold values from 0.5 to 1.5
- query_weight: bfloat16 [1536, 1536], P('ctx'), may hold values from -0.15625 to 0.15625
- key_matrix: bfloat16 [1536, 512], P('ctx'), may hold values from -0.15625 to 0.15625
- value_matrix: bfloat16 [1536, 512], P('ctx'), may hold values from -0.15625 to 0.15625
- output_matrix: bfloat16 [1536, 1536], P('ctx'), may hold values from -0.3125 to 0.3125
- ffn_gain: bfloat16 [1536], P('ctx'), may hold values from 0.5 to 1.5
- router_weight: bfloat16 [1536, 40], P('ctx')
- gateup_weight: bfloat16 [40, 1536, 1024], P('expert'), may hold values from -0.15625 to 0.15625
- down_weight: bfloat16 [40, 512, 1536], P('expert'), may hold values from -0.375 to 0.375
Outputs:
- output: bfloat16 [4, 4096, 1536], P('expert', 'ctx')
- input_grad: bfloat16 [4, 4096, 1536], P('expert', 'ctx')
- attn_gain_grad: float32 [1536], P('ctx')
- query_grad: float32 [1536, 1536], P('ctx')
- key_grad: float32 [1536, 512], P('ctx')
- value_grad: float32 [1536, 512], P('ctx')
- outproj_grad: float32 [1536, 1536], P('ctx')
- ffn_gain_grad: float32 [1536], P('ctx')
- router_grad: float32 [1536, 40], P('ctx')
- gateup_grad: float32 [40, 1536, 1024], P('expert', 'ctx')
- down_grad: float32 [40, 512, 1536], P('expert', None, 'ctx')
The draws below stay inside these ranges and needn't reach their ends.
Inputs may be any that keep to these rules, and one draw needn't show every extreme that they name: `routes`: each row names 8 different experts. In each block of 512 positions of a sequence no expert is named by more than 128 rows, and in some blocks one is named by exactly 128 rows.
All inputs are finite; a program needn't handle non-finite values.
Results may differ from the reference program's by a relative error of at most 0.025.
Values may be sent and summed in bfloat16 or wider, within the bound.
No kernel may reach another device: no remote copies, remote signals or barrier semaphores. Data moves between devices by JAX's collectives and lax.ppermute only.
A program may use at most 448 MiB of HBM per device.

```python
import math
import jax
import jax.numpy as jnp
import numpy as np
from jax import lax

MODEL_WIDTH = 1536
QUERY_HEADS = 24
KEY_VALUE_HEADS = 8
HEAD_SIZE = 64
FFE = 512
EXPERTS = 40
TOPK = 8
SEQUENCE_LENGTH = 4096
SEQS = 4
CH = 512
CAP = 128


def draw_router_weight(key, part):
    first_term, second_term = jax.random.split(jax.random.fold_in(key, 202))
    base = jnp.clip(jax.random.normal(first_term, (MODEL_WIDTH, EXPERTS), jnp.float32), -6.0, 6.0) / jnp.sqrt(jnp.float32(MODEL_WIDTH))
    spread = jnp.exp(jax.random.uniform(second_term, (EXPERTS,), jnp.float32, 0.0, jnp.log(6.0)))
    return (base * spread[None, :]).astype(jnp.bfloat16)


def block_scale(rng, shape, cuts, smallest, high):
    def one(dim, parts):
        steps = jax.random.uniform(jax.random.fold_in(jax.random.fold_in(rng, 6), dim), (parts,), jnp.float32, smallest / len(cuts), high / len(cuts))
        return jnp.repeat(jnp.exp(steps), shape[dim] // parts).reshape((-1,) + (1,) * (len(shape) - dim - 1))

    loudness = one(*cuts[0])
    for cut in cuts[1:]:
        loudness = loudness * one(*cut)
    return loudness


def assign_block(rng, own, number, rows, number_of, top, reach, skew):
    order = jax.random.permutation(rng, number_of)
    crowded, usual = load_shares(number_of, rows * top, reach, skew, True), load_shares(number_of, rows * top, reach, skew, False)
    places = jnp.arange(number_of)

    def named(tallies, turn):
        used = int((tallies > 0).sum())
        fixed = max(1, used // 4)
        moved = fixed + (places - fixed + turn * (used - fixed)) % max(1, number_of - fixed)
        return jnp.zeros((number_of,), jnp.int32).at[order[jnp.where(places < fixed, places, moved)]].set(jnp.asarray(tallies, jnp.int32))

    tallies = jnp.where(number % 4 == 0, named(crowded, number // 4), named(usual, number - number // 4 - 1))
    mixed = jax.random.permutation(jax.random.fold_in(own, 3), number_of)
    giver, taker = mixed[0:number_of // 2 * 2:2], mixed[1:number_of // 2 * 2:2]
    slack = jnp.minimum(tallies[giver] - 1, reach - tallies[taker]) // 2
    slack = jnp.where((giver == order[0]) | (taker == order[0]) | (tallies[taker] == 0), 0, jnp.maximum(slack, 0))
    moved = jax.random.randint(jax.random.fold_in(own, 4), (number_of // 2,), 0, 1 << 20) % (slack + 1)
    tallies = tallies.at[giver].add(-moved).at[taker].add(moved)
    items = jnp.searchsorted(jnp.cumsum(tallies), jnp.arange(rows * top), side="right").astype(jnp.int32)
    listing = items.reshape(top, rows).T
    listing = listing[jax.random.permutation(jax.random.fold_in(own, 1), rows)]
    turn = jax.random.randint(jax.random.fold_in(own, 2), (rows, 1), 0, top)
    return jnp.take_along_axis(listing, (jnp.arange(top)[None, :] + turn) % top, axis=1)


def load_shares(count, total, reach, skew, full):
    loads = [(1 << 20) // math.isqrt(grade ** skew) + 1 for grade in range(1, count + 1)]
    largest = reach if full else min(reach, max(-(-total // count), total * loads[0] // sum(loads)))
    least = 1 if total - largest >= count - 1 else 0
    counts, rest = [largest] + [least] * (count - 1), total - largest - least * (count - 1)
    while rest > 0:
        free = [i for i in range(1, count) if counts[i] < largest] or [i for i in range(1, count) if counts[i] < reach]
        mass, left = sum([loads[i] for i in free]), rest
        for i in free:
            extra = min(reach - counts[i], max(1, left * loads[i] // mass), rest)
            counts[i] = counts[i] + extra
            rest = rest - extra
    return np.array(counts)


def bell_draw(own_key, shape, width, most, cuts=(), kind=jnp.bfloat16):
    factor_of = block_scale(own_key, shape, cuts, -0.22, 0.18) if cuts else 1.0
    array = jax.random.normal(own_key, shape, jnp.float32) * width * factor_of
    return jnp.minimum(jnp.maximum(array, -most), most).astype(kind)


def setup_inputs(seed: int = 0) -> dict:
    seeds = jax.random.split(jax.random.key(seed), 13)
    inputs = bell_draw(seeds[0], (SEQS, SEQUENCE_LENGTH, MODEL_WIDTH), 1.0, 6.0, ((0, 4), (1, 8)))
    cotangent = bell_draw(seeds[1], (SEQS, SEQUENCE_LENGTH, MODEL_WIDTH), 1.0, 6.0, ((0, 4), (1, 8)))
    routes_keys = jax.random.split(jax.random.fold_in(seeds[2], 1), SEQS * SEQUENCE_LENGTH // CH)
    routes_turns = jax.random.permutation(jax.random.fold_in(seeds[2], 3), SEQS * SEQUENCE_LENGTH // CH)
    routes = jax.vmap(lambda own, number: assign_block(jax.random.fold_in(seeds[2], 2), own, number, CH, EXPERTS, TOPK, CAP, 2))(routes_keys, routes_turns).reshape((SEQS, SEQUENCE_LENGTH, TOPK))
    attn_gain = jnp.clip(1.0 + 0.1 * jax.random.normal(seeds[3], (MODEL_WIDTH,), jnp.float32), 0.5, 1.5).astype(jnp.bfloat16)
    query_weight = bell_draw(seeds[4], (MODEL_WIDTH, QUERY_HEADS * HEAD_SIZE), MODEL_WIDTH ** -0.5, 0.15625, ((0, 8),))
    key_matrix = bell_draw(seeds[5], (MODEL_WIDTH, KEY_VALUE_HEADS * HEAD_SIZE), MODEL_WIDTH ** -0.5, 0.15625, ((0, 8),))
    value_matrix = bell_draw(seeds[6], (MODEL_WIDTH, KEY_VALUE_HEADS * HEAD_SIZE), MODEL_WIDTH ** -0.5, 0.15625, ((0, 8),))
    output_matrix = bell_draw(seeds[7], (QUERY_HEADS * HEAD_SIZE, MODEL_WIDTH), (max(QUERY_HEADS * HEAD_SIZE // 4, 4)) ** -0.5, 0.3125, ((0, 8),))
    ffn_gain = jnp.clip(1.0 + 0.1 * jax.random.normal(seeds[8], (MODEL_WIDTH,), jnp.float32), 0.5, 1.5).astype(jnp.bfloat16)
    router_weight = draw_router_weight(jax.random.fold_in(seeds[12], 71), 0)
    gateup_weight = bell_draw(seeds[10], (EXPERTS, MODEL_WIDTH, 2 * FFE), MODEL_WIDTH ** -0.5, 0.15625, ((0, 4),))
    down_weight = bell_draw(seeds[11], (EXPERTS, FFE, MODEL_WIDTH), (max(FFE // 2, 4)) ** -0.5, 0.375, ((0, 4),))
    return dict(inputs=inputs, cotangent=cotangent, routes=routes, attn_gain=attn_gain, query_weight=query_weight, key_matrix=key_matrix, value_matrix=value_matrix, output_matrix=output_matrix, ffn_gain=ffn_gain, router_weight=router_weight, gateup_weight=gateup_weight, down_weight=down_weight)


EPS = 1e-05
NEG = -1e+30
THETA = 10000.0

def lowered_precision(values):
    return lax.optimization_barrier(values.astype(jnp.bfloat16))

def norm_rows(values, gain):
    factor = lax.rsqrt(lax.optimization_barrier(jnp.mean(values * values, axis=-1, keepdims=True)) + EPS)
    return (values * factor * gain, factor)

def norm_back(grad_norm, values, factor, gain):
    gain_grad = lax.optimization_barrier(jnp.sum(grad_norm * values * factor, axis=0))
    inner = grad_norm * gain
    part = factor * inner - values * factor ** 3 * lax.optimization_barrier(jnp.mean(inner * values, axis=-1, keepdims=True))
    return (gain_grad, part)

def angles(positions):
    half = HEAD_SIZE // 2
    freq = jnp.power(THETA, -jnp.arange(half).astype(positions.dtype) / half)
    turned = positions[:, None] * freq[None, :]
    return (jnp.cos(turned)[:, None, :], jnp.sin(turned)[:, None, :])

def rotary_tables(values, cosine_table, sine_table):
    half = values.shape[-1] // 2
    first_term = values[..., :half]
    second_term = values[..., half:]
    return jnp.concatenate([first_term * cosine_table - second_term * sine_table, second_term * cosine_table + first_term * sine_table], axis=-1)

def sequence_pass(tokens, grad_in, route_seq, params):
    attn_gain, query_weight, key_matrix, value_matrix, output_matrix, ffn_gain, router_weight, gateup_weight, down_weight = params
    single_float = jnp.float32
    query_groups = QUERY_HEADS // KEY_VALUE_HEADS
    scale = HEAD_SIZE ** (-0.5)
    gain_one = attn_gain.astype(single_float)
    gain_two = ffn_gain.astype(single_float)
    flat_in = tokens.astype(single_float)
    product, rms_one = norm_rows(flat_in, gain_one)
    normalized_input = lowered_precision(product)
    cosine_table, sine_table = angles(jnp.arange(SEQUENCE_LENGTH).astype(single_float))
    query_unrotated = jnp.dot(normalized_input, query_weight, preferred_element_type=single_float).reshape(SEQUENCE_LENGTH, QUERY_HEADS, HEAD_SIZE)
    query_rows = lowered_precision(rotary_tables(query_unrotated, cosine_table, sine_table)).reshape(SEQUENCE_LENGTH, KEY_VALUE_HEADS, query_groups, HEAD_SIZE)
    key_unrotated = jnp.dot(normalized_input, key_matrix, preferred_element_type=single_float).reshape(SEQUENCE_LENGTH, KEY_VALUE_HEADS, HEAD_SIZE)
    key_rows = lowered_precision(rotary_tables(key_unrotated, cosine_table, sine_table))
    value_matrix_rows = lowered_precision(jnp.dot(normalized_input, value_matrix, preferred_element_type=single_float)).reshape(SEQUENCE_LENGTH, KEY_VALUE_HEADS, HEAD_SIZE)
    key_f = key_rows.astype(single_float)
    value_f = value_matrix_rows.astype(single_float)
    position_block = min(512, SEQUENCE_LENGTH)
    blocks = SEQUENCE_LENGTH // position_block
    key_pos = jnp.arange(SEQUENCE_LENGTH, dtype=jnp.int32)

    def forward_block(number):
        start = number * position_block
        query_part = lax.dynamic_slice_in_dim(query_rows, start, position_block, 0).astype(single_float)
        query_pos = start + jnp.arange(position_block, dtype=jnp.int32)
        allowed = (key_pos[None, :] <= query_pos[:, None])[:, None, None, :]
        scores = jnp.einsum('qngd,knd->qngk', query_part, key_f) * scale
        scores = jnp.where(allowed, scores, NEG)
        peak = lax.optimization_barrier(jnp.max(scores, axis=-1))
        weights = jnp.where(allowed, jnp.exp(scores - peak[..., None]), 0.0)
        total_w = lax.optimization_barrier(jnp.sum(weights, axis=-1))
        mixed = jnp.einsum('qngk,knd->qngd', lowered_precision(weights).astype(single_float), value_f)
        return (lowered_precision(mixed / total_w[..., None]), peak + jnp.log(total_w))
    attention_result, log_sum_exponent = lax.map(forward_block, jnp.arange(blocks, dtype=jnp.int32))
    attention_result = attention_result.reshape(SEQUENCE_LENGTH, KEY_VALUE_HEADS, query_groups, HEAD_SIZE)
    log_sum_exponent = log_sum_exponent.reshape(SEQUENCE_LENGTH, KEY_VALUE_HEADS, query_groups)
    flat_att = attention_result.reshape(SEQUENCE_LENGTH, QUERY_HEADS * HEAD_SIZE)
    hidden = flat_in + jnp.dot(flat_att, output_matrix, preferred_element_type=single_float)
    product_two, rms_two = norm_rows(hidden, gain_two)
    normed_two = lowered_precision(product_two)
    logits = jnp.dot(normed_two, router_weight, preferred_element_type=single_float)
    picks = route_seq[..., None] == jnp.arange(EXPERTS, dtype=jnp.int32)
    chosen = lax.optimization_barrier(jnp.sum(jnp.where(picks, logits[:, None, :], 0.0), axis=-1))
    probs = jax.nn.softmax(chosen, axis=-1)
    spans = SEQUENCE_LENGTH // CH
    assigned = route_seq.reshape(spans, CH * TOPK)
    hits = (assigned[..., None] == jnp.arange(EXPERTS, dtype=jnp.int32)).astype(jnp.int32)
    rank = lax.optimization_barrier(jnp.sum((jnp.cumsum(hits, axis=1) - hits) * hits, axis=-1))
    slots = ((assigned * spans + jnp.arange(spans, dtype=jnp.int32)[:, None]) * CAP + rank).reshape(-1)
    sources = jnp.arange(SEQUENCE_LENGTH * TOPK, dtype=jnp.int32) // TOPK
    buffer_rows = EXPERTS * spans * CAP
    inbound = jnp.zeros((buffer_rows, MODEL_WIDTH), jnp.bfloat16).at[slots].set(normed_two[sources]).reshape(EXPERTS, spans * CAP, MODEL_WIDTH)

    def expert_forward(args):
        arrived, gate_up, down = args
        mixed = jnp.dot(arrived, gate_up, preferred_element_type=single_float)
        gate_val = mixed[:, :FFE]
        up_val = mixed[:, FFE:]
        activ = lowered_precision(gate_val * jax.nn.sigmoid(gate_val) * up_val)
        result = lowered_precision(jnp.dot(activ, down, preferred_element_type=single_float))
        return (result, mixed, activ)
    expert_out, mixed_all, activ_all = lax.map(expert_forward, (inbound, gateup_weight, down_weight))
    per_route = expert_out.reshape(buffer_rows, MODEL_WIDTH)[slots].reshape(SEQUENCE_LENGTH, TOPK, MODEL_WIDTH).astype(single_float)
    combined = lax.optimization_barrier(jnp.sum(probs[..., None] * per_route, axis=1))
    output = (hidden + combined).astype(jnp.bfloat16)
    grad = grad_in.astype(single_float)
    route_grad = lax.optimization_barrier(jnp.sum(grad[:, None, :] * per_route, axis=-1))
    sent_grad = lowered_precision(probs[..., None] * grad[:, None, :]).reshape(SEQUENCE_LENGTH * TOPK, MODEL_WIDTH)
    grad_buffer = jnp.zeros((buffer_rows, MODEL_WIDTH), jnp.bfloat16).at[slots].set(sent_grad).reshape(EXPERTS, spans * CAP, MODEL_WIDTH)

    def expert_backward(args):
        arrived, grads_here, mixed_here, activ_here, gate_up, down = args
        act_grad = jnp.dot(grads_here, down.T, preferred_element_type=single_float)
        gate_val = mixed_here[:, :FFE]
        up_val = mixed_here[:, FFE:]
        logistic = jax.nn.sigmoid(gate_val)
        mix_grad = lowered_precision(jnp.concatenate([act_grad * up_val * logistic * (1.0 + gate_val * (1.0 - logistic)), act_grad * gate_val * logistic], axis=-1))
        down_part = jnp.dot(activ_here.T, grads_here, preferred_element_type=single_float)
        gate_part = jnp.dot(arrived.T, mix_grad, preferred_element_type=single_float)
        back_rows = lowered_precision(jnp.dot(mix_grad, gate_up.T, preferred_element_type=single_float))
        return (back_rows, gate_part, down_part)
    back_all, gateup_part, down_part = lax.map(expert_backward, (inbound, grad_buffer, mixed_all, activ_all, gateup_weight, down_weight))
    normed_two_grad = lax.optimization_barrier(jnp.sum(back_all.reshape(buffer_rows, MODEL_WIDTH)[slots].reshape(SEQUENCE_LENGTH, TOPK, MODEL_WIDTH).astype(single_float), axis=1))
    chosen_grad = probs * (route_grad - lax.optimization_barrier(jnp.sum(probs * route_grad, axis=-1, keepdims=True)))
    logit_grad = lowered_precision(lax.optimization_barrier(jnp.sum(jnp.where(picks, chosen_grad[..., None], 0.0), axis=1)))
    router_part = jnp.dot(normed_two.T, logit_grad, preferred_element_type=single_float)
    normed_two_grad = normed_two_grad + jnp.dot(logit_grad, router_weight.T, preferred_element_type=single_float)
    ffn_gain_part, hidden_part = norm_back(normed_two_grad, hidden, rms_two, gain_two)
    hidden_grad = grad + hidden_part
    hidden_reduced = lowered_precision(hidden_grad)
    outproj_part = jnp.dot(flat_att.T, hidden_reduced, preferred_element_type=single_float)
    attention_result_grad = lowered_precision(jnp.dot(hidden_reduced, output_matrix.T, preferred_element_type=single_float)).reshape(SEQUENCE_LENGTH, KEY_VALUE_HEADS, query_groups, HEAD_SIZE)
    delta = lax.optimization_barrier(jnp.sum(attention_result_grad.astype(single_float) * attention_result.astype(single_float), axis=-1))

    def backward_block(carry, number):
        key_acc, value_acc = carry
        start = number * position_block
        query_part = lax.dynamic_slice_in_dim(query_rows, start, position_block, 0).astype(single_float)
        grad_part = lax.dynamic_slice_in_dim(attention_result_grad, start, position_block, 0).astype(single_float)
        lse_part = lax.dynamic_slice_in_dim(log_sum_exponent, start, position_block, 0)
        delta_part = lax.dynamic_slice_in_dim(delta, start, position_block, 0)
        query_pos = start + jnp.arange(position_block, dtype=jnp.int32)
        allowed = (key_pos[None, :] <= query_pos[:, None])[:, None, None, :]
        scores = jnp.einsum('qngd,knd->qngk', query_part, key_f) * scale
        scores = jnp.where(allowed, scores, NEG)
        prob_full = jnp.where(allowed, jnp.exp(scores - lse_part[..., None]), 0.0)
        prob_low = lowered_precision(prob_full).astype(single_float)
        value_acc = value_acc + jnp.einsum('qngk,qngd->knd', prob_low, grad_part)
        dots = jnp.einsum('qngd,knd->qngk', grad_part, value_f)
        score_grad = lowered_precision(prob_full * (dots - delta_part[..., None]) * scale).astype(single_float)
        query_sum = jnp.einsum('qngk,knd->qngd', score_grad, key_f)
        key_acc = key_acc + jnp.einsum('qngk,qngd->knd', score_grad, query_part)
        return ((key_acc, value_acc), query_sum)
    initial_accumulator = (jnp.zeros((SEQUENCE_LENGTH, KEY_VALUE_HEADS, HEAD_SIZE), single_float), jnp.zeros((SEQUENCE_LENGTH, KEY_VALUE_HEADS, HEAD_SIZE), single_float))
    (key_total, value_total), query_sum = lax.scan(backward_block, initial_accumulator, jnp.arange(blocks, dtype=jnp.int32))
    query_sum = query_sum.reshape(SEQUENCE_LENGTH, QUERY_HEADS, HEAD_SIZE)
    query_back = lowered_precision(rotary_tables(query_sum, cosine_table, -sine_table)).reshape(SEQUENCE_LENGTH, QUERY_HEADS * HEAD_SIZE)
    key_backward = lowered_precision(rotary_tables(key_total, cosine_table, -sine_table)).reshape(SEQUENCE_LENGTH, KEY_VALUE_HEADS * HEAD_SIZE)
    value_backward = lowered_precision(value_total).reshape(SEQUENCE_LENGTH, KEY_VALUE_HEADS * HEAD_SIZE)
    query_part_w = jnp.dot(normalized_input.T, query_back, preferred_element_type=single_float)
    key_part_w = jnp.dot(normalized_input.T, key_backward, preferred_element_type=single_float)
    value_part_w = jnp.dot(normalized_input.T, value_backward, preferred_element_type=single_float)
    normed_one_grad = jnp.dot(query_back, query_weight.T, preferred_element_type=single_float)
    normed_one_grad = normed_one_grad + jnp.dot(key_backward, key_matrix.T, preferred_element_type=single_float)
    normed_one_grad = normed_one_grad + jnp.dot(value_backward, value_matrix.T, preferred_element_type=single_float)
    attn_gain_part, input_part = norm_back(normed_one_grad, flat_in, rms_one, gain_one)
    input_grad = (hidden_grad + input_part).astype(jnp.bfloat16)
    grads = (attn_gain_part, query_part_w, key_part_w, value_part_w, outproj_part, ffn_gain_part, router_part, gateup_part, down_part)
    return (output, input_grad, grads)

def reference(inputs, cotangent, routes, attn_gain, query_weight, key_matrix, value_matrix, output_matrix, ffn_gain, router_weight, gateup_weight, down_weight):
    params = (attn_gain, query_weight, key_matrix, value_matrix, output_matrix, ffn_gain, router_weight, gateup_weight, down_weight)
    start_sums = tuple((jnp.zeros(item.shape, jnp.float32) for item in params))

    def visit(carry, item):
        out_seq, grad_seq, grads = sequence_pass(item[0], item[1], item[2], params)
        return (tuple((left + right for left, right in zip(carry, grads))), (out_seq, grad_seq))
    totals, stacked = lax.scan(visit, start_sums, (inputs, cotangent, routes))
    return (stacked[0], stacked[1], totals[0], totals[1], totals[2], totals[3], totals[4], totals[5], totals[6], totals[7], totals[8])
```

```python
import functools

import jax
import jax.numpy as jnp
from jax import lax
from jax.experimental import pallas as pl
from jax.experimental.pallas import tpu as pltpu
from jax.sharding import PartitionSpec as P

QUERY_HEADS = 24
KEY_VALUE_HEADS = 8
HEAD_SIZE = 64
GROUP = QUERY_HEADS // KEY_VALUE_HEADS
QROWS = GROUP * HEAD_SIZE
SLICE = QROWS + 2 * HEAD_SIZE
FFE = 512
EXPERTS = 40
TOPK = 8
EXTRA = 128

EPS = 1e-05
NEG = -1e30
THETA = 10000.0

F32 = jnp.float32
BF16 = jnp.bfloat16
VMEM_LIMIT = 60 * 1024 * 1024
COST = pl.CostEstimate(flops=1024, bytes_accessed=1024, transcendentals=0)


def contract(left, right, a, b):
    return lax.dot_general(left, right, (((a,), (b,)), ((), ())), preferred_element_type=F32)


def params(*order):
    return pltpu.CompilerParams(vmem_limit_bytes=VMEM_LIMIT, dimension_semantics=order)


def whole(*shape):
    return pl.BlockSpec(shape, lambda *_: (0,) * len(shape))


def project_kernel(x_ref, gain_ref, w_ref, table_ref, *refs):
    n_ref, q_ref, kv_ref = refs[-3:]
    half = HEAD_SIZE // 2
    x = x_ref[0].astype(F32)
    factor = lax.rsqrt(jnp.mean(x * x, axis=-1, keepdims=True) + EPS)
    normed = (x * factor * gain_ref[...]).astype(BF16)
    n_ref[0] = normed
    raw = contract(w_ref[...], normed, 1, 1)
    cosine, sine = table_ref[0, :half], table_ref[0, half:]
    scale = HEAD_SIZE**-0.5
    for g in range(GROUP + 1):
        a, b = raw[g * HEAD_SIZE : g * HEAD_SIZE + half], raw[g * HEAD_SIZE + half : (g + 1) * HEAD_SIZE]
        turned = jnp.concatenate([a * cosine - b * sine, b * cosine + a * sine], axis=0).astype(BF16)
        if g < GROUP:
            q_ref[0, g * HEAD_SIZE : (g + 1) * HEAD_SIZE, :] = turned * BF16(scale)
        else:
            kv_ref[0, :HEAD_SIZE, :] = turned
    kv_ref[0, HEAD_SIZE:, :] = raw[QROWS + HEAD_SIZE :].astype(BF16)


def project(x, gain, w_rows, table, which, held):
    blocks, columns, width = x.shape
    span = table.shape[2]
    shapes = [(blocks, span, width), (blocks, QROWS, span), (blocks, 2 * HEAD_SIZE, span)]
    return pl.pallas_call(
        project_kernel,
        grid=(blocks,),
        in_specs=[
            pl.BlockSpec((1, columns, width), lambda b: (b, 0, 0)),
            whole(1, width),
            whole(SLICE, width),
            pl.BlockSpec((1, HEAD_SIZE, columns), lambda b: (b, 0, which)),
        ]
        + [pl.BlockSpec(memory_space=pl.ANY)] * len(held),
        out_specs=[
            pl.BlockSpec((1, columns, width), lambda b: (b, which, 0)),
            pl.BlockSpec((1, QROWS, columns), lambda b: (b, 0, which)),
            pl.BlockSpec((1, 2 * HEAD_SIZE, columns), lambda b: (b, 0, which)),
        ],
        out_shape=[jax.ShapeDtypeStruct(shape, BF16) for shape in shapes],
        input_output_aliases={4 + i: i for i in range(len(held))},
        compiler_params=params("arbitrary"),
        cost_estimate=COST,
        name="project",
    )(x, gain, w_rows, table, *held)


def head_grads_kernel(back_ref, n_ref, grad_ref, acc):
    b = pl.program_id(0)
    part = contract(n_ref[0], back_ref[0], 0, 1)

    @pl.when(b == 0)
    def _():
        acc[...] = part

    @pl.when(b > 0)
    def _():
        acc[...] += part

    @pl.when(b == pl.num_programs(0) - 1)
    def _():
        grad_ref[...] = acc[...].astype(BF16)


def head_grads(back, normed):
    blocks, rows, span = back.shape
    width = normed.shape[2]
    return pl.pallas_call(
        head_grads_kernel,
        grid=(blocks,),
        in_specs=[
            pl.BlockSpec((1, rows, span), lambda b: (b, 0, 0)),
            pl.BlockSpec((1, span, width), lambda b: (b, 0, 0)),
        ],
        out_specs=whole(width, rows),
        out_shape=jax.ShapeDtypeStruct((width, rows), BF16),
        scratch_shapes=[pltpu.VMEM((width, rows), F32)],
        compiler_params=params("arbitrary"),
        cost_estimate=COST,
        name="head_grads",
    )(back, normed)


def key_tiles(first, count, sub, span, part, bk):
    low = (first // sub) * span + part * sub + first % sub
    last = first + count - 1
    high = (last // sub) * span + part * sub + last % sub
    return (low + 1) // bk, (high + bk) // bk


def loop(first, last, step):
    def body(j, carry):
        step(j)
        return carry

    lax.fori_loop(first, last, body, 0)


def unpack_blocks(refs, out):
    groups, size, _ = out.shape
    for i in range(refs.shape[0]):
        columns = refs.shape[2]
        for g in range(groups):
            out[g, :, i * columns : (i + 1) * columns] = refs[i, g * size : (g + 1) * size, :]


def attend_kernel(bk, sub, span, part_ref, pos_ref, q_ref, kv_ref, o_ref, lse_ref, q, keys, values, peak, total, acc):
    groups, size, bq = q.shape
    tile = pl.program_id(0)

    @pl.when(tile == 0)
    def _():
        for i in range(kv_ref.shape[0]):
            part = slice(i * span, (i + 1) * span)
            keys[part, :] = jnp.transpose(kv_ref[i, :size, :], (1, 0))
            values[:, part] = kv_ref[i, size:, :]

    unpack_blocks(q_ref, q)
    unmasked, ends = key_tiles(tile * bq, bq, sub, span, part_ref[0], bk)
    peak[...] = jnp.full(peak.shape, NEG, F32)
    total[...] = jnp.zeros(total.shape, F32)
    acc[...] = jnp.zeros(acc.shape, F32)

    def step(j, masked):
        start = pl.multiple_of(j * bk, bk)
        k = keys[pl.ds(start, bk), :]
        v = values[:, pl.ds(start, bk)]
        if masked:
            allowed = (start + lax.broadcasted_iota(jnp.int32, (bk, bq), 0)) <= pos_ref[...]
        for g in range(groups):
            scores = jnp.dot(k, q[g], preferred_element_type=F32)
            if masked:
                scores = jnp.where(allowed, scores, NEG)
            old = peak[g]
            new = jnp.maximum(old, jnp.max(scores, axis=0, keepdims=True))
            weights = jnp.exp(scores - new)
            factor = jnp.exp(old - new)
            peak[g] = new
            total[g] = total[g] * factor + jnp.sum(weights, axis=0, keepdims=True)
            acc[g] = acc[g] * factor + jnp.dot(v, weights.astype(BF16), preferred_element_type=F32)

    loop(0, unmasked, lambda j: step(j, False))
    loop(unmasked, ends, lambda j: step(j, True))
    for g in range(groups):
        out = (acc[g] / total[g]).astype(BF16)
        lse_ref[g] = peak[g] + jnp.log(total[g])
        for i in range(o_ref.shape[0]):
            o_ref[i, g * size : (g + 1) * size, :] = out[:, i * o_ref.shape[2] : (i + 1) * o_ref.shape[2]]


def attend(part, pos, q, kv, bq, bk, sub, span):
    nq, blocks = pos.shape[1], pos.shape[1] // sub
    nk = blocks * span
    groups, size, rows = GROUP, HEAD_SIZE, QROWS
    tile = pl.BlockSpec((bq // sub, rows, sub), lambda i: (i, 0, 0))
    stat = pl.BlockSpec((groups, 1, bq), lambda i: (0, 0, i))
    return pl.pallas_call(
        functools.partial(attend_kernel, bk, sub, span),
        grid=(nq // bq,),
        in_specs=[
            pl.BlockSpec(memory_space=pltpu.SMEM),
            pl.BlockSpec((1, bq), lambda i: (0, i)),
            tile,
            whole(blocks, 2 * size, span),
        ],
        out_specs=[tile, stat],
        out_shape=[
            jax.ShapeDtypeStruct((blocks, rows, sub), BF16),
            jax.ShapeDtypeStruct((groups, 1, nq), F32),
        ],
        scratch_shapes=[
            pltpu.VMEM((groups, size, bq), BF16),
            pltpu.VMEM((nk, size), BF16),
            pltpu.VMEM((size, nk), BF16),
            pltpu.VMEM((groups, 1, bq), F32),
            pltpu.VMEM((groups, 1, bq), F32),
            pltpu.VMEM((groups, size, bq), F32),
        ],
        compiler_params=params("arbitrary"),
        cost_estimate=COST,
        name="attend",
    )(part, pos, q, kv)


def turn_back(rows, cosine, sine):
    half = HEAD_SIZE // 2
    a, b = rows[:half], rows[half:]
    return jnp.concatenate([a * cosine + b * sine, b * cosine - a * sine], axis=0)


def attend_back_kernel(
    bk, sub, span, part_ref, pos_ref, q_ref, o_ref, do_ref, lse_ref, kv_ref, qtab_ref, ktab_ref, *refs
):
    *outs, q, keys, keys_t, values, q_rows, do, do_rows, delta, dq, dk, dv = refs
    dq_ref, dkv_ref = outs[0], outs[-1]
    groups, size, bq = q.shape
    half = size // 2
    tile = pl.program_id(0)

    @pl.when(tile == 0)
    def _():
        for i in range(kv_ref.shape[0]):
            part = slice(i * span, (i + 1) * span)
            keys[part, :] = jnp.transpose(kv_ref[i, :size, :], (1, 0))
            keys_t[:, part] = kv_ref[i, :size, :]
            values[part, :] = jnp.transpose(kv_ref[i, size:, :], (1, 0))
        dk[...] = jnp.zeros(dk.shape, F32)
        dv[...] = jnp.zeros(dv.shape, F32)

    unpack_blocks(q_ref, q)
    unpack_blocks(do_ref, do)
    pieces, columns = do_ref.shape[0], do_ref.shape[2]
    for g in range(groups):
        for i in range(pieces):
            both = do_ref[i, g * size : (g + 1) * size, :].astype(F32) * o_ref[i, g * size : (g + 1) * size, :].astype(F32)
            delta[g, :, i * columns : (i + 1) * columns] = jnp.sum(both, axis=0, keepdims=True)
        q_rows[g] = jnp.transpose(q[g], (1, 0))
        do_rows[g] = jnp.transpose(do[g], (1, 0))
    dq[...] = jnp.zeros(dq.shape, F32)
    unmasked, ends = key_tiles(tile * bq, bq, sub, span, part_ref[0], bk)

    def step(j, masked):
        start = pl.multiple_of(j * bk, bk)
        k = keys[pl.ds(start, bk), :]
        kt = keys_t[:, pl.ds(start, bk)]
        v = values[pl.ds(start, bk), :]
        if masked:
            allowed = (start + lax.broadcasted_iota(jnp.int32, (bk, bq), 0)) <= pos_ref[...]
        dv_part = jnp.zeros((bk, size), F32)
        dk_part = jnp.zeros((bk, size), F32)
        for g in range(groups):
            scores = jnp.dot(k, q[g], preferred_element_type=F32)
            prob = jnp.exp(scores - lse_ref[g])
            if masked:
                prob = jnp.where(allowed, prob, 0.0)
            dv_part = dv_part + jnp.dot(prob.astype(BF16), do_rows[g], preferred_element_type=F32)
            dots = jnp.dot(v, do[g], preferred_element_type=F32)
            score_grad = (prob * (dots - delta[g])).astype(BF16)
            dk_part = dk_part + jnp.dot(score_grad, q_rows[g], preferred_element_type=F32)
            dq[g] += jnp.dot(kt, score_grad, preferred_element_type=F32)
        dv[pl.ds(start, bk), :] += dv_part
        dk[pl.ds(start, bk), :] += dk_part

    loop(0, unmasked, lambda j: step(j, False))
    loop(unmasked, ends, lambda j: step(j, True))
    scale = HEAD_SIZE**-0.5
    packed = len(outs) == 1
    for i in range(pieces):
        cols = slice(i * columns, (i + 1) * columns)
        for g in range(groups):
            out = turn_back(dq[g, :, cols], qtab_ref[i, :half], qtab_ref[i, half:])
            dq_ref[tile if packed else i, g * size : (g + 1) * size, :] = (out * scale).astype(BF16)

    @pl.when(tile == pl.num_programs(0) - 1)
    def _():
        base = QROWS if packed else 0
        for i in range(dkv_ref.shape[0]):
            part = slice(i * span, (i + 1) * span)
            back = turn_back(jnp.transpose(dk[part, :], (1, 0)), ktab_ref[i, :half], ktab_ref[i, half:])
            dkv_ref[i, base : base + size, :] = back.astype(BF16)
            dkv_ref[i, base + size : base + 2 * size, :] = jnp.transpose(dv[part, :], (1, 0)).astype(BF16)


def attend_back(part, pos, q, o, do, lse, kv, qtab, ktab, bq, bk, sub, span):
    nq, blocks = pos.shape[1], pos.shape[1] // sub
    nk = blocks * span
    groups, size, rows = GROUP, HEAD_SIZE, QROWS
    tile = pl.BlockSpec((bq // sub, rows, sub), lambda i: (i, 0, 0))
    if sub == span == bq:
        out_specs = [whole(blocks, SLICE, span)]
        out_shape = [jax.ShapeDtypeStruct((blocks, SLICE, span), BF16)]
    else:
        out_specs = [tile, whole(blocks, 2 * size, span)]
        out_shape = [
            jax.ShapeDtypeStruct((blocks, rows, sub), BF16),
            jax.ShapeDtypeStruct((blocks, 2 * size, span), BF16),
        ]
    return pl.pallas_call(
        functools.partial(attend_back_kernel, bk, sub, span),
        grid=(nq // bq,),
        in_specs=[
            pl.BlockSpec(memory_space=pltpu.SMEM),
            pl.BlockSpec((1, bq), lambda i: (0, i)),
            tile,
            tile,
            tile,
            pl.BlockSpec((groups, 1, bq), lambda i: (0, 0, i)),
            whole(blocks, 2 * size, span),
            pl.BlockSpec((bq // sub, size, sub), lambda i: (i, 0, 0)),
            whole(blocks, size, span),
        ],
        out_specs=out_specs,
        out_shape=out_shape,
        scratch_shapes=[
            pltpu.VMEM((groups, size, bq), BF16),
            pltpu.VMEM((nk, size), BF16),
            pltpu.VMEM((size, nk), BF16),
            pltpu.VMEM((nk, size), BF16),
            pltpu.VMEM((groups, bq, size), BF16),
            pltpu.VMEM((groups, size, bq), BF16),
            pltpu.VMEM((groups, bq, size), BF16),
            pltpu.VMEM((groups, 1, bq), F32),
            pltpu.VMEM((groups, size, bq), F32),
            pltpu.VMEM((nk, size), F32),
            pltpu.VMEM((nk, size), F32),
        ],
        compiler_params=params("arbitrary"),
        cost_estimate=COST,
        name="attend_back",
    )(part, pos, q, o, do, lse, kv, qtab, ktab)


def chosen_rows(rank, cap):
    return lax.broadcasted_iota(jnp.int32, (cap, rank.shape[1]), 0) == rank


def dispatch_kernel(cap, rank_ref, token_ref, row_ref):
    for e in range(rank_ref.shape[0]):
        one = chosen_rows(rank_ref[e], cap).astype(F32).astype(BF16)
        row_ref[e] = jnp.dot(one, token_ref[...], preferred_element_type=F32).astype(BF16)


def dispatch(rank, tokens, block, cap, wide):
    count = rank.shape[0]
    span, width = tokens.shape
    return pl.pallas_call(
        functools.partial(dispatch_kernel, cap),
        grid=(width // wide,),
        in_specs=[
            pl.BlockSpec((count, 1, span), lambda i: (0, 0, block)),
            pl.BlockSpec((span, wide), lambda i: (0, i)),
        ],
        out_specs=pl.BlockSpec((count, cap, wide), lambda i: (0, 0, i)),
        out_shape=jax.ShapeDtypeStruct((count, cap, width), BF16),
        compiler_params=params("arbitrary"),
        cost_estimate=COST,
        name="dispatch",
    )(rank, tokens)


def experts_kernel(span, cap, offset, blocks, place_ref, rank_ref, prob_ref, *refs):
    x_refs, g_refs = refs[:blocks], refs[blocks : 2 * blocks]
    gu_ref, dn_ref, back_ref, out_ref, mine_ref, theirs_ref, grads = refs[2 * blocks :]
    e = pl.program_id(0)
    x = jnp.concatenate([ref[0] for ref in x_refs], axis=0)
    g = jnp.concatenate([ref[0] for ref in g_refs], axis=0)
    width = x.shape[1]
    ps = []
    for i in range(blocks):
        rows = slice(i * span, (i + 1) * span)
        hit = chosen_rows(rank_ref[0, :, rows], cap)
        ps.append(jnp.sum(jnp.where(hit, prob_ref[0, :, rows], 0.0), axis=1, keepdims=True))
    prob = jnp.concatenate(ps, axis=0)
    mixed = jnp.dot(x, gu_ref[0], preferred_element_type=F32)
    gate, up = mixed[:, :FFE], mixed[:, FFE:]
    logistic = 1.0 / (1.0 + jnp.exp(-gate))
    act = (gate * logistic * up).astype(BF16)
    sent = (prob * g.astype(F32)).astype(BF16)
    act_grad = contract(sent, dn_ref[0], 1, 1)
    mix = jnp.concatenate(
        [act_grad * up * logistic * (1.0 + gate * (1.0 - logistic)), act_grad * gate * logistic], axis=1
    ).astype(BF16)
    out = jnp.dot(act, dn_ref[0], preferred_element_type=F32).astype(BF16).astype(F32)
    route = jnp.sum(g.astype(F32) * out, axis=1, keepdims=True)
    out_ref[0] = (prob * out).astype(BF16)
    back_ref[0, :, :width] = contract(mix, gu_ref[0], 1, 1).astype(BF16)
    high = route.astype(BF16).astype(F32)
    place = lax.broadcasted_iota(jnp.int32, (route.shape[0], EXTRA), 1) - (place_ref[0] + offset + e)
    extra = jnp.where(place == 0, high, jnp.where(place == EXPERTS, route - high, 0.0))
    back_ref[0, :, width:] = extra.astype(BF16)
    grads[:, : 2 * FFE] = contract(x, mix, 0, 0).astype(BF16)
    grads[:, 2 * FFE :] = contract(sent, act, 0, 0).astype(BF16)
    pairs, _, own, _ = mine_ref.shape
    core = place_ref[1]
    for i in range(pairs):
        mine_ref[i, 0] = grads[pl.ds(pl.multiple_of((2 * i + core) * own, own), own), :]
        theirs_ref[i, 0] = grads[pl.ds(pl.multiple_of((2 * i + 1 - core) * own, own), own), :]


def run_experts(place, rank, prob, xs, gs, gateup, down, offset, count, n_ctx, span, cap):
    blocks = len(xs)
    width = gateup.shape[1]
    rows = blocks * cap
    tokens = blocks * span
    own = width // n_ctx
    pairs = n_ctx // 2

    def picked(*shape):
        return pl.BlockSpec((1,) + shape, lambda e: (e + offset, 0, 0))

    def row(wide):
        return pl.BlockSpec((1, rows, wide), lambda e: (e, 0, 0))

    half = pl.BlockSpec((pairs, 1, own, 3 * FFE), lambda e: (0, e, 0, 0))
    half_shape = jax.ShapeDtypeStruct((pairs, count, own, 3 * FFE), BF16)
    return pl.pallas_call(
        functools.partial(experts_kernel, span, cap, offset, blocks),
        grid=(count,),
        in_specs=[pl.BlockSpec(memory_space=pltpu.SMEM), picked(1, tokens), picked(1, tokens)]
        + [picked(cap, width)] * (2 * blocks)
        + [picked(width, 2 * FFE), picked(FFE, width)],
        out_specs=[row(width + EXTRA), row(width), half, half],
        out_shape=[
            jax.ShapeDtypeStruct((count, rows, width + EXTRA), BF16),
            jax.ShapeDtypeStruct((count, rows, width), BF16),
            half_shape,
            half_shape,
        ],
        scratch_shapes=[pltpu.VMEM((width, 3 * FFE), BF16)],
        compiler_params=params("arbitrary"),
        cost_estimate=COST,
        name="experts",
    )(place, rank, prob, *xs, *gs, gateup, down)


def unpack_kernel(sum_ref, *refs):
    gateup_ref, down_ref = refs[-2:]
    gateup_ref[0] = sum_ref[0, :, : 2 * FFE].astype(F32)
    down_ref[0] = jnp.transpose(sum_ref[0, :, 2 * FFE :].astype(F32), (1, 0))


def unpack(total, offset, experts, held):
    count, own, wide = total.shape
    return pl.pallas_call(
        unpack_kernel,
        grid=(count,),
        in_specs=[pl.BlockSpec((1, own, wide), lambda e: (e, 0, 0))] + [pl.BlockSpec(memory_space=pl.ANY)] * len(held),
        out_specs=[
            pl.BlockSpec((1, own, 2 * FFE), lambda e: (e + offset, 0, 0)),
            pl.BlockSpec((1, FFE, own), lambda e: (e + offset, 0, 0)),
        ],
        out_shape=[
            jax.ShapeDtypeStruct((experts, own, 2 * FFE), F32),
            jax.ShapeDtypeStruct((experts, FFE, own), F32),
        ],
        input_output_aliases={1 + i: i for i in range(len(held))},
        compiler_params=params("arbitrary"),
        cost_estimate=COST,
        name="unpack",
    )(total, *held)


def combine_kernel(cap, n_parts, *refs):
    rank_refs, row_refs, out_ref = refs[:n_parts], refs[n_parts : 2 * n_parts], refs[-1]
    total = None
    for rank_ref, row_ref in zip(rank_refs, row_refs):
        ones, rows = [], []
        for e in range(rank_ref.shape[0]):
            ones.append(chosen_rows(rank_ref[e], cap).astype(F32).astype(BF16))
            rows.append(row_ref[e])
        part = contract(jnp.concatenate(ones, axis=0), jnp.concatenate(rows, axis=0), 0, 0)
        total = part if total is None else total + part
    out_ref[...] = total.astype(BF16)


def combine(ranks, rows, block, span, cap, wide):
    width = rows[0].shape[2]
    count = sum(r.shape[0] for r in ranks)
    return pl.pallas_call(
        functools.partial(combine_kernel, cap, len(ranks)),
        grid=(width // wide,),
        in_specs=[pl.BlockSpec((r.shape[0], 1, span), lambda i: (0, 0, block)) for r in ranks]
        + [pl.BlockSpec((r.shape[0], cap, wide), lambda i: (0, block, i)) for r in rows],
        out_specs=pl.BlockSpec((span, wide), lambda i: (0, i)),
        out_shape=jax.ShapeDtypeStruct((span, width), BF16),
        compiler_params=params("arbitrary"),
        cost_estimate=COST,
        name="combine",
    )(*ranks, *rows)


def swapped(array, axis, mask):
    count = lax.axis_size(axis)
    return lax.ppermute(array, axis, [(i, i ^ mask) for i in range(count)])


def gather_blocks(array, axis):
    count = lax.axis_size(axis)
    if count != 4:
        return [array] + [swapped(array, axis, k) for k in range(1, count)]
    half = array.shape[0] // 2
    one, two = swapped(array, axis, 1), swapped(array, axis, 2)
    far = jnp.concatenate([swapped(two[:half], axis, 1), swapped(one[half:], axis, 2)], axis=0)
    return [array, one, two, far]


def gather_start(array, axis):
    return [array, swapped(array, axis, 1), swapped(array, axis, 2)]


def gather_end(array, one, two, axis):
    count = lax.axis_size(axis)
    if count != 4:
        return [array, one, two] + [swapped(array, axis, k) for k in range(3, count)]
    half = array.shape[0] // 2
    far = jnp.concatenate([swapped(two[:half], axis, 1), swapped(one[half:], axis, 2)], axis=0)
    return [array, one, two, far]


def gather_rows(array, axis, use, early):
    count = lax.axis_size(axis)
    if count != 4:
        return [use(block, k) for k, block in enumerate(gather_blocks(array, axis))], early
    half = array.shape[0] // 2
    one, two = swapped(array, axis, 1), swapped(array, axis, 2)
    own = use(array, 0)
    own, one, two, early = lax.optimization_barrier((own, one, two, early))
    far = jnp.concatenate([swapped(two[:half], axis, 1), swapped(one[half:], axis, 2)], axis=0)
    return [own, use(one, 1), use(two, 2), use(far, 3)], early


def wide_sum(*arrays):
    return sum(array.astype(F32) for array in arrays)


def return_start(parts, axis):
    if lax.axis_size(axis) != 4:
        return [parts[0]] + [swapped(parts[k], axis, k) for k in range(1, len(parts))]
    own, one, two, far = parts
    half = own.shape[0] // 2
    via_one, via_two = swapped(far[:half], axis, 1), swapped(far[half:], axis, 2)
    return [own, one, two, via_one, via_two, swapped(one[:half], axis, 1), swapped(two[half:], axis, 2)]


def return_end(held, axis):
    if lax.axis_size(axis) != 4:
        return wide_sum(*held)
    own, one, two, via_one, via_two, one_low, two_high = held
    half = own.shape[0] // 2
    one_high = swapped(wide_sum(one[half:], via_two).astype(BF16), axis, 1)
    two_low = swapped(wide_sum(two[:half], via_one).astype(BF16), axis, 2)
    return jnp.concatenate(
        [wide_sum(own[:half], one_low, two_low), wide_sum(own[half:], one_high, two_high)], axis=0
    )


def for_partners(array, axis, dim):
    count, me = lax.axis_size(axis), lax.axis_index(axis)
    return [lax.dynamic_index_in_dim(array, me ^ k, dim, keepdims=False) for k in range(count)]


def sum_from_partners(parts, axis):
    return wide_sum(parts[0], *[swapped(parts[k], axis, k) for k in range(1, len(parts))]).astype(BF16)


def in_order(blocks, axis):
    me = lax.axis_index(axis)
    blocks = jnp.stack(blocks)
    return jnp.stack([lax.dynamic_index_in_dim(blocks, me ^ k, 0, keepdims=False) for k in range(blocks.shape[0])])


def all_of_expert(array):
    count = lax.axis_size("expert")
    return in_order([array] + [swapped(array, "expert", k) for k in range(1, count)], "expert")


def norm_rows(values, gain):
    factor = lax.rsqrt(jnp.mean(values * values, axis=-1, keepdims=True) + EPS)
    return (values * factor * gain).astype(BF16), factor


def norm_back(grad_norm, values, factor, gain):
    inner = grad_norm * gain
    return factor * inner - values * factor**3 * jnp.mean(inner * values, axis=-1, keepdims=True)


def angles(positions):
    half = HEAD_SIZE // 2
    freq = jnp.power(THETA, -jnp.arange(half).astype(F32) / half)
    turned = freq[None, :, None] * positions.astype(F32)[:, None, :]
    return jnp.concatenate([jnp.cos(turned), jnp.sin(turned)], axis=1)


def per_device(
    inputs,
    cotangent,
    routes,
    attn_gain,
    query_weight,
    key_matrix,
    value_matrix,
    output_matrix,
    ffn_gain,
    router_weight,
    gateup_weight,
    down_weight,
):
    _, span, width = inputs.shape
    n_ctx = lax.axis_size("ctx")
    n_owner = lax.axis_size("expert")
    own_rows = query_weight.shape[0]
    local_experts = gateup_weight.shape[0]
    cap = span // 4
    parts = n_ctx // KEY_VALUE_HEADS
    sub = span // parts
    part = lax.axis_index("ctx") % parts
    part_arg = part.astype(jnp.int32).reshape(1)

    tokens_in = inputs.reshape(span, width)
    me = lax.axis_index("expert")
    piece = own_rows // n_owner

    def a_part(array):
        return lax.dynamic_slice_in_dim(array, me * piece, piece, 0)

    heads = jnp.concatenate(
        [
            a_part(query_weight).reshape(piece, KEY_VALUE_HEADS, QROWS),
            a_part(key_matrix).reshape(piece, KEY_VALUE_HEADS, HEAD_SIZE),
            a_part(value_matrix).reshape(piece, KEY_VALUE_HEADS, HEAD_SIZE),
        ],
        axis=-1,
    ).transpose(1, 0, 2)
    small = jnp.concatenate([attn_gain[:, None], ffn_gain[:, None], router_weight], axis=1)
    small = a_part(jnp.pad(small, ((0, 0), (0, HEAD_SIZE - small.shape[1]))))
    sends = jnp.concatenate(
        [jnp.repeat(heads, parts, axis=0), jnp.broadcast_to(small[None], (n_ctx,) + small.shape)], axis=-1
    )
    weights = all_of_expert(lax.all_to_all(sends, "ctx", 0, 0, tiled=True))
    weights = weights.transpose(1, 0, 2, 3).reshape(width, -1)
    head_weight = weights[:, :SLICE].T
    gain_one = weights[:, SLICE].astype(F32)
    gain_two = weights[:, SLICE + 1].astype(F32)
    router = weights[:, SLICE + 2 : SLICE + 2 + EXPERTS]

    names = routes.reshape(span, TOPK)
    hits = jnp.any(names[:, :, None] == jnp.arange(EXPERTS), axis=1)
    upto = (jnp.arange(span)[:, None] <= jnp.arange(span)[None, :]).astype(BF16)
    counted = contract(hits.astype(BF16), upto, 0, 0)
    ranks = jnp.where(hits.T, counted - 1.0, -1.0).astype(BF16)

    def to_owners(array):
        array = lax.all_to_all(array.reshape(n_owner, local_experts, span), "expert", 0, 0, tiled=True)
        blocks = [lax.dynamic_index_in_dim(array, me ^ k, 0, keepdims=False) for k in range(n_owner)]
        return jnp.concatenate(blocks, axis=1)[:, None]

    every = jnp.arange(n_ctx * span, dtype=jnp.int32).reshape(n_ctx, span)
    table = angles(every)
    pieces = 2
    x_pieces = [
        lax.all_gather(piece, "ctx", axis=0, tiled=False)
        for piece in jnp.split(tokens_in, pieces, axis=0)
    ]
    grad_in = cotangent.reshape(span, width)
    held = gather_start(grad_in, "expert")
    rank = to_owners(ranks)
    x_pieces[0], held, head_weight, rank = lax.optimization_barrier((x_pieces[0], held, head_weight, rank))
    rank = rank.astype(jnp.int32)
    grad_blocks = gather_end(*held, "expert")
    buffers = project(x_pieces[0], gain_one[None], head_weight, table, 0, ())
    x_pieces[1], grad_blocks, buffers = lax.optimization_barrier((x_pieces[1], grad_blocks, buffers))
    normed_all, q_all, kv_all = project(x_pieces[1], gain_one[None], head_weight, table, 1, buffers)
    if parts == 1:
        queries, positions, q_table = q_all, every, table
    else:

        def mine(array):
            array = array.reshape(array.shape[:-1] + (parts, sub))
            return lax.dynamic_index_in_dim(array, part, array.ndim - 2, keepdims=False)

        queries, positions, q_table = mine(q_all), mine(every), mine(table)
    pos = positions.reshape(1, -1)

    output_matrix, w_heads, queries = lax.optimization_barrier((output_matrix, head_weight, queries))
    w_output = lax.all_gather(output_matrix, "ctx", axis=0, tiled=True)
    grad_rows = [dispatch(rank, block, k, cap, width // 2) for k, block in enumerate(grad_blocks)]
    tile = min(512, n_ctx * sub)
    attended, lse = attend(part_arg, pos, queries, kv_all, tile, tile, sub, span)

    def to_rows(array):
        array = lax.all_to_all(array, "ctx", 0, 0, tiled=True)
        array = array.reshape(KEY_VALUE_HEADS, parts, -1, sub).transpose(0, 2, 1, 3)
        return array.reshape(-1, span)

    attended_rows, grad_rows = lax.optimization_barrier((to_rows(attended), grad_rows))
    flat_in = tokens_in.astype(F32)
    hidden = flat_in + contract(attended_rows, w_output, 0, 0)
    normed_two, rms_two = norm_rows(hidden, gain_two)
    w_heads, normed_two = lax.optimization_barrier((w_heads, normed_two))
    w_heads = lax.all_gather(w_heads, "ctx", axis=0, tiled=False)[::parts].reshape(-1, width)
    logits = jnp.dot(normed_two, router, preferred_element_type=F32)
    masked = jnp.where(hits, logits, NEG)
    powers = jnp.where(hits, jnp.exp(masked - jnp.max(masked, axis=-1, keepdims=True)), 0.0)
    probs = powers / jnp.sum(powers, axis=-1, keepdims=True)
    prob = to_owners(probs.T)

    place = jnp.stack([me * local_experts, lax.axis_index("ctx") % 2]).astype(jnp.int32)
    token_rows, prob = gather_rows(
        normed_two, "expert", lambda block, k: dispatch(rank, block, k, cap, width // 2), prob
    )
    cuts, offset = [], 0
    for count in (1, 1, 3, 3, local_experts):
        if offset < local_experts:
            cuts.append((offset, min(count, local_experts - offset)))
            offset += count
    backs, outs, sums = [], [], []
    core_line = [[z * 2 + core for z in range(n_ctx // 2)] for core in range(2)]

    def pair_sum(mine, theirs):
        return wide_sum(mine, swapped(theirs, "ctx", 1)).astype(BF16)

    def line_sum(pair):
        total = lax.psum_scatter(
            pair.reshape(-1, 3 * FFE), "ctx", scatter_dimension=0, tiled=True, axis_index_groups=core_line
        )
        return total.reshape(-1, own_rows, 3 * FFE)

    for number, (offset, count) in enumerate(cuts):
        back, out, mine, theirs = run_experts(
            place, rank, prob, token_rows, grad_rows, gateup_weight, down_weight, offset, count, n_ctx, span, cap
        )
        backs.append(back)
        outs.append(out)
        if number < len(cuts) - 1:
            sums.append(line_sum(pair_sum(mine, theirs)))
            if number == 1:
                w_heads, place = lax.optimization_barrier((w_heads, place))
    ranks = [rank[offset : offset + count] for offset, count in cuts]

    def to_tokens(rows):
        return [combine(ranks, rows, k, span, cap, rows[0].shape[2]) for k in reversed(range(n_owner))][::-1]

    back_sum = return_end(return_start(to_tokens(backs), "expert"), "expert")

    grad = cotangent.reshape(span, width).astype(F32)
    route_grad = back_sum[:, width : width + EXPERTS] + back_sum[:, width + EXPERTS : width + 2 * EXPERTS]
    chosen_grad = probs * (route_grad - jnp.sum(probs * route_grad, axis=-1, keepdims=True))
    logit_grad = chosen_grad.astype(BF16)
    router_full = contract(normed_two, logit_grad, 0, 0)
    normed_two_grad = back_sum[:, :width] + contract(logit_grad, router, 1, 1)
    ffn_gain_full = jnp.sum(normed_two_grad * hidden * rms_two, axis=0)
    hidden_grad = grad + norm_back(normed_two_grad, hidden, rms_two, gain_two)
    hidden_low = hidden_grad.astype(BF16)
    attended_grad = contract(w_output, hidden_low, 1, 1).astype(BF16)
    attended_grad = attended_grad.reshape(KEY_VALUE_HEADS, QROWS, parts, sub).transpose(0, 2, 1, 3)
    attended_grad = lax.all_to_all(attended_grad.reshape(n_ctx, QROWS, sub), "ctx", 0, 0, tiled=True)
    outproj_full = jnp.dot(attended_rows, hidden_low, preferred_element_type=F32)
    column = jnp.arange(EXTRA)[None]
    side = jnp.where(
        column == EXPERTS, ffn_gain_full[:, None], jnp.pad(router_full, ((0, 0), (0, EXTRA - EXPERTS)))
    ).astype(BF16)
    mixed_full = jnp.concatenate([outproj_full.astype(BF16), lax.optimization_barrier(side)], axis=1)

    mixed_parts = for_partners(mixed_full.reshape(n_ctx, n_owner, -1, mixed_full.shape[1]), "expert", 1)
    theirs, hidden_low = lax.optimization_barrier((theirs, hidden_low))
    pair, outs, mixed_parts = lax.optimization_barrier((pair_sum(mine, theirs), outs, mixed_parts))
    mixed_part = sum_from_partners(mixed_parts, "expert")
    out_parts = return_start(to_tokens(outs), "expert")
    out_parts, attended_grad, mixed_part = lax.optimization_barrier((out_parts, attended_grad, mixed_part))
    mixed_part = lax.all_to_all(mixed_part, "ctx", 0, 0, tiled=True)
    backs = attend_back(
        part_arg, pos, queries, attended, attended_grad, lse, kv_all, q_table, table, tile, tile, sub, span
    )
    mixed_part, backs = lax.optimization_barrier((mixed_part, backs))
    output = hidden + return_end(out_parts, "expert")
    output = output.astype(BF16).reshape(1, span, width)
    if len(backs) == 1:
        rows_back = lax.all_to_all(backs[0], "ctx", 0, 0, tiled=True).reshape(-1, span)
        head_grad = head_grads(backs[0], normed_all)
    else:
        query_back, kv_back = backs
        query_rows = to_rows(query_back).reshape(KEY_VALUE_HEADS, QROWS, span)
        kv_rows = lax.all_to_all(kv_back, "ctx", 0, 0, tiled=True).astype(F32)
        kv_rows = jnp.sum(kv_rows.reshape(KEY_VALUE_HEADS, parts, 2 * HEAD_SIZE, span), axis=1).astype(BF16)
        rows_back = jnp.concatenate([query_rows, kv_rows], axis=1).reshape(-1, span)
        normed_part = normed_all.reshape(n_ctx, parts, sub, width)
        normed_part = lax.dynamic_index_in_dim(normed_part, part, 1, keepdims=False)
        head_grad = jnp.concatenate([head_grads(query_back, normed_part), head_grads(kv_back, normed_all)], axis=1)
    head_parts = for_partners(head_grad.reshape(n_ctx, n_owner, -1, SLICE), "expert", 1)
    head_part = sum_from_partners(head_parts, "expert")
    pair, rows_back, head_part = lax.optimization_barrier((pair, rows_back, head_part))
    head_part = lax.all_to_all(head_part, "ctx", 0, 0, tiled=True)
    sums.append(line_sum(pair))
    grads = ()
    for (offset, _), total in zip(cuts, sums):
        grads = unpack(total, offset, local_experts, grads)
    gateup_grad, down_grad = grads
    mixed_sum = jnp.sum(mixed_part.astype(F32), axis=0).astype(BF16)
    head_sum = jnp.sum(head_part.astype(F32).reshape(KEY_VALUE_HEADS, parts, -1, SLICE), axis=1).astype(BF16)
    head_sum = head_sum.transpose(1, 0, 2).reshape(-1, KEY_VALUE_HEADS * SLICE)
    last = all_of_expert(jnp.concatenate([mixed_sum, head_sum], axis=1)).reshape(own_rows, -1).astype(F32)
    mixed_sum = last[:, : -KEY_VALUE_HEADS * SLICE]
    head_grad = last[:, -KEY_VALUE_HEADS * SLICE :].reshape(own_rows, KEY_VALUE_HEADS, SLICE)
    normed_one_grad = contract(rows_back, w_heads, 0, 0)
    rms_one = lax.rsqrt(jnp.mean(flat_in * flat_in, axis=-1, keepdims=True) + EPS)
    input_grad = (
        (hidden_grad + norm_back(normed_one_grad, flat_in, rms_one, gain_one)).astype(BF16).reshape(1, span, width)
    )

    outproj_grad = mixed_sum[:, :width]
    router_grad = mixed_sum[:, width : width + EXPERTS]
    ffn_gain_grad = mixed_sum[:, width + EXPERTS]
    query_grad = head_grad[..., :QROWS].reshape(own_rows, -1)
    key_grad = head_grad[..., QROWS : QROWS + HEAD_SIZE].reshape(own_rows, -1)
    value_grad = head_grad[..., QROWS + HEAD_SIZE :].reshape(own_rows, -1)
    attn_gain_grad = (
        jnp.sum(query_weight.astype(F32) * query_grad, axis=1)
        + jnp.sum(key_matrix.astype(F32) * key_grad, axis=1)
        + jnp.sum(value_matrix.astype(F32) * value_grad, axis=1)
    ) / attn_gain.astype(F32)
    return (
        output,
        input_grad,
        attn_gain_grad,
        query_grad,
        key_grad,
        value_grad,
        outproj_grad,
        ffn_gain_grad,
        router_grad,
        gateup_grad,
        down_grad,
    )


def solution(mesh):
    tokens = P("expert", "ctx", None)
    row = P("ctx")
    rows = P("ctx", None)
    owned = P("expert", None, None)
    return jax.shard_map(
        per_device,
        mesh=mesh,
        in_specs=(tokens, tokens, tokens, row, rows, rows, rows, rows, row, rows, owned, owned),
        out_specs=(
            tokens,
            tokens,
            row,
            rows,
            rows,
            rows,
            rows,
            row,
            rows,
            P("expert", "ctx", None),
            P("expert", None, "ctx"),
        ),
        check_vma=False,
    )
```

```python
import functools

import jax
import jax.numpy as jnp
from jax import lax
from jax.experimental import pallas as pl
from jax.experimental.pallas import tpu as pltpu
from jax.sharding import PartitionSpec as P

QUERY_HEADS = 24
KEY_VALUE_HEADS = 8
HEAD_SIZE = 64
GROUP = QUERY_HEADS // KEY_VALUE_HEADS
QROWS = GROUP * HEAD_SIZE
SLICE = QROWS + 2 * HEAD_SIZE
FFE = 512
EXPERTS = 40
TOPK = 8
EXTRA = 128

EPS = 1e-05
NEG = -1e30
THETA = 10000.0

F32 = jnp.float32
BF16 = jnp.bfloat16
VMEM_LIMIT = 60 * 1024 * 1024
COST = pl.CostEstimate(flops=1024, bytes_accessed=1024, transcendentals=0)


def contract(left, right, a, b):
    return lax.dot_general(left, right, (((a,), (b,)), ((), ())), preferred_element_type=F32)


def params(*order):
    return pltpu.CompilerParams(vmem_limit_bytes=VMEM_LIMIT, dimension_semantics=order)


def whole(*shape):
    return pl.BlockSpec(shape, lambda *_: (0,) * len(shape))


def project_kernel(x_ref, gain_ref, w_ref, table_ref, *refs):
    n_ref, q_ref, kv_ref = refs[-3:]
    half = HEAD_SIZE // 2
    x = x_ref[0].astype(F32)
    factor = lax.rsqrt(jnp.mean(x * x, axis=-1, keepdims=True) + EPS)
    normed = (x * factor * gain_ref[...]).astype(BF16)
    n_ref[0] = normed
    raw = contract(w_ref[...], normed, 1, 1)
    cosine, sine = table_ref[0, :half], table_ref[0, half:]
    scale = HEAD_SIZE**-0.5
    for g in range(GROUP + 1):
        a, b = raw[g * HEAD_SIZE : g * HEAD_SIZE + half], raw[g * HEAD_SIZE + half : (g + 1) * HEAD_SIZE]
        turned = jnp.concatenate([a * cosine - b * sine, b * cosine + a * sine], axis=0).astype(BF16)
        if g < GROUP:
            q_ref[0, g * HEAD_SIZE : (g + 1) * HEAD_SIZE, :] = turned * BF16(scale)
        else:
            kv_ref[0, :HEAD_SIZE, :] = turned
    kv_ref[0, HEAD_SIZE:, :] = raw[QROWS + HEAD_SIZE :].astype(BF16)


def project(x, gain, w_rows, table, which, held):
    blocks, columns, width = x.shape
    span = table.shape[2]
    shapes = [(blocks, span, width), (blocks, QROWS, span), (blocks, 2 * HEAD_SIZE, span)]
    return pl.pallas_call(
        project_kernel,
        grid=(blocks,),
        in_specs=[
            pl.BlockSpec((1, columns, width), lambda b: (b, 0, 0)),
            whole(1, width),
            whole(SLICE, width),
            pl.BlockSpec((1, HEAD_SIZE, columns), lambda b: (b, 0, which)),
        ]
        + [pl.BlockSpec(memory_space=pl.ANY)] * len(held),
        out_specs=[
            pl.BlockSpec((1, columns, width), lambda b: (b, which, 0)),
            pl.BlockSpec((1, QROWS, columns), lambda b: (b, 0, which)),
            pl.BlockSpec((1, 2 * HEAD_SIZE, columns), lambda b: (b, 0, which)),
        ],
        out_shape=[jax.ShapeDtypeStruct(shape, BF16) for shape in shapes],
        input_output_aliases={4 + i: i for i in range(len(held))},
        compiler_params=params("arbitrary"),
        cost_estimate=COST,
        name="project",
    )(x, gain, w_rows, table, *held)


def head_grads_kernel(back_ref, n_ref, grad_ref, acc):
    b = pl.program_id(0)
    part = contract(n_ref[0], back_ref[0], 0, 1)

    @pl.when(b == 0)
    def _():
        acc[...] = part

    @pl.when(b > 0)
    def _():
        acc[...] += part

    @pl.when(b == pl.num_programs(0) - 1)
    def _():
        grad_ref[...] = acc[...].astype(BF16)


def head_grads(back, normed):
    blocks, rows, span = back.shape
    width = normed.shape[2]
    return pl.pallas_call(
        head_grads_kernel,
        grid=(blocks,),
        in_specs=[
            pl.BlockSpec((1, rows, span), lambda b: (b, 0, 0)),
            pl.BlockSpec((1, span, width), lambda b: (b, 0, 0)),
        ],
        out_specs=whole(width, rows),
        out_shape=jax.ShapeDtypeStruct((width, rows), BF16),
        scratch_shapes=[pltpu.VMEM((width, rows), F32)],
        compiler_params=params("arbitrary"),
        cost_estimate=COST,
        name="head_grads",
    )(back, normed)


def key_tiles(first, count, sub, span, part, bk):
    low = (first // sub) * span + part * sub + first % sub
    last = first + count - 1
    high = (last // sub) * span + part * sub + last % sub
    return (low + 1) // bk, (high + bk) // bk


def loop(first, last, step):
    def body(j, carry):
        step(j)
        return carry

    lax.fori_loop(first, last, body, 0)


def unpack_blocks(refs, out):
    groups, size, _ = out.shape
    for i in range(refs.shape[0]):
        columns = refs.shape[2]
        for g in range(groups):
            out[g, :, i * columns : (i + 1) * columns] = refs[i, g * size : (g + 1) * size, :]


def attend_kernel(
    bk, sub, span, part_ref, pos_ref, q_ref, kv_ref, o_ref, lse_ref, q, keys, values, peak, total, acc, highest
):
    groups, size, bq = q.shape
    tile = pl.program_id(0)

    @pl.when(tile == 0)
    def _():
        for i in range(kv_ref.shape[0]):
            part = slice(i * span, (i + 1) * span)
            keys[part, :] = jnp.transpose(kv_ref[i, :size, :], (1, 0))
            values[:, part] = kv_ref[i, size:, :]

    unpack_blocks(q_ref, q)
    unmasked, ends = key_tiles(tile * bq, bq, sub, span, part_ref[0], bk)

    def reset():
        peak[...] = jnp.full(peak.shape, NEG, F32)
        total[...] = jnp.zeros(total.shape, F32)
        acc[...] = jnp.zeros(acc.shape, F32)

    def step(j, masked, moving):
        start = pl.multiple_of(j * bk, bk)
        k = keys[pl.ds(start, bk), :]
        v = values[:, pl.ds(start, bk)]
        if masked:
            allowed = (start + lax.broadcasted_iota(jnp.int32, (bk, bq), 0)) <= pos_ref[...]

        def score(g):
            scores = jnp.dot(k, q[g], preferred_element_type=F32)
            return jnp.where(allowed, scores, NEG) if masked else scores

        ahead = score(0)
        for g in range(groups):
            scores = ahead
            if g + 1 < groups:
                ahead = score(g + 1)
            old = peak[g]
            most = jnp.max(scores, axis=0, keepdims=True)
            if moving:
                new = jnp.maximum(old, most)
                factor = jnp.exp(old - new)
                peak[g] = new
                total[g] = total[g] * factor
                acc[g] = acc[g] * factor
            else:
                new = old
                highest[g] = jnp.maximum(highest[g], most)
            weights = jnp.exp(scores - new)
            total[g] += jnp.sum(weights, axis=0, keepdims=True)
            acc[g] += jnp.dot(v, weights.astype(BF16), preferred_element_type=F32)

    reset()
    loop(unmasked, ends, lambda j: step(j, True, True))
    highest[...] = peak[...]
    loop(0, unmasked, lambda j: step(j, False, False))

    @pl.when(jnp.max(highest[...] - peak[...]) > 30.0)
    def _():
        reset()
        loop(0, unmasked, lambda j: step(j, False, True))
        loop(unmasked, ends, lambda j: step(j, True, True))

    for g in range(groups):
        out = (acc[g] / total[g]).astype(BF16)
        lse_ref[g] = peak[g] + jnp.log(total[g])
        for i in range(o_ref.shape[0]):
            o_ref[i, g * size : (g + 1) * size, :] = out[:, i * o_ref.shape[2] : (i + 1) * o_ref.shape[2]]


def attend(part, pos, q, kv, bq, bk, sub, span):
    nq, blocks = pos.shape[1], pos.shape[1] // sub
    nk = blocks * span
    groups, size, rows = GROUP, HEAD_SIZE, QROWS
    tile = pl.BlockSpec((bq // sub, rows, sub), lambda i: (i, 0, 0))
    stat = pl.BlockSpec((groups, 1, bq), lambda i: (0, 0, i))
    return pl.pallas_call(
        functools.partial(attend_kernel, bk, sub, span),
        grid=(nq // bq,),
        in_specs=[
            pl.BlockSpec(memory_space=pltpu.SMEM),
            pl.BlockSpec((1, bq), lambda i: (0, i)),
            tile,
            whole(blocks, 2 * size, span),
        ],
        out_specs=[tile, stat],
        out_shape=[
            jax.ShapeDtypeStruct((blocks, rows, sub), BF16),
            jax.ShapeDtypeStruct((groups, 1, nq), F32),
        ],
        scratch_shapes=[
            pltpu.VMEM((groups, size, bq), BF16),
            pltpu.VMEM((nk, size), BF16),
            pltpu.VMEM((size, nk), BF16),
            pltpu.VMEM((groups, 1, bq), F32),
            pltpu.VMEM((groups, 1, bq), F32),
            pltpu.VMEM((groups, size, bq), F32),
            pltpu.VMEM((groups, 1, bq), F32),
        ],
        compiler_params=params("arbitrary"),
        cost_estimate=COST,
        name="attend",
    )(part, pos, q, kv)


def turn_back(rows, cosine, sine):
    half = HEAD_SIZE // 2
    a, b = rows[:half], rows[half:]
    return jnp.concatenate([a * cosine + b * sine, b * cosine - a * sine], axis=0)


def attend_back_kernel(
    bk, sub, span, part_ref, pos_ref, q_ref, o_ref, do_ref, lse_ref, kv_ref, qtab_ref, ktab_ref, *refs
):
    *outs, q, keys, keys_t, values, q_rows, do, do_rows, delta, dq, dk, dv = refs
    dq_ref, dkv_ref = outs[0], outs[-1]
    groups, size, bq = q.shape
    half = size // 2
    tile = pl.program_id(0)

    @pl.when(tile == 0)
    def _():
        for i in range(kv_ref.shape[0]):
            part = slice(i * span, (i + 1) * span)
            keys[part, :] = jnp.transpose(kv_ref[i, :size, :], (1, 0))
            keys_t[:, part] = kv_ref[i, :size, :]
            values[part, :] = jnp.transpose(kv_ref[i, size:, :], (1, 0))
        dk[...] = jnp.zeros(dk.shape, F32)
        dv[...] = jnp.zeros(dv.shape, F32)

    unpack_blocks(q_ref, q)
    unpack_blocks(do_ref, do)
    pieces, columns = do_ref.shape[0], do_ref.shape[2]
    for g in range(groups):
        for i in range(pieces):
            both = do_ref[i, g * size : (g + 1) * size, :].astype(F32) * o_ref[i, g * size : (g + 1) * size, :].astype(F32)
            delta[g, :, i * columns : (i + 1) * columns] = jnp.sum(both, axis=0, keepdims=True)
        q_rows[g] = jnp.transpose(q[g], (1, 0))
        do_rows[g] = jnp.transpose(do[g], (1, 0))
    dq[...] = jnp.zeros(dq.shape, F32)
    unmasked, ends = key_tiles(tile * bq, bq, sub, span, part_ref[0], bk)

    def step(j, masked):
        start = pl.multiple_of(j * bk, bk)
        k = keys[pl.ds(start, bk), :]
        kt = keys_t[:, pl.ds(start, bk)]
        v = values[pl.ds(start, bk), :]
        if masked:
            allowed = (start + lax.broadcasted_iota(jnp.int32, (bk, bq), 0)) <= pos_ref[...]
        dv_part = jnp.zeros((bk, size), F32)
        dk_part = jnp.zeros((bk, size), F32)
        for g in range(groups):
            scores = jnp.dot(k, q[g], preferred_element_type=F32)
            prob = jnp.exp(scores - lse_ref[g])
            if masked:
                prob = jnp.where(allowed, prob, 0.0)
            dv_part = dv_part + jnp.dot(prob.astype(BF16), do_rows[g], preferred_element_type=F32)
            dots = jnp.dot(v, do[g], preferred_element_type=F32)
            score_grad = (prob * (dots - delta[g])).astype(BF16)
            dk_part = dk_part + jnp.dot(score_grad, q_rows[g], preferred_element_type=F32)
            dq[g] += jnp.dot(kt, score_grad, preferred_element_type=F32)
        dv[pl.ds(start, bk), :] += dv_part
        dk[pl.ds(start, bk), :] += dk_part

    loop(0, unmasked, lambda j: step(j, False))
    loop(unmasked, ends, lambda j: step(j, True))
    scale = HEAD_SIZE**-0.5
    packed = len(outs) == 1
    for i in range(pieces):
        cols = slice(i * columns, (i + 1) * columns)
        for g in range(groups):
            out = turn_back(dq[g, :, cols], qtab_ref[i, :half], qtab_ref[i, half:])
            dq_ref[tile if packed else i, g * size : (g + 1) * size, :] = (out * scale).astype(BF16)

    @pl.when(tile == pl.num_programs(0) - 1)
    def _():
        base = QROWS if packed else 0
        for i in range(dkv_ref.shape[0]):
            part = slice(i * span, (i + 1) * span)
            back = turn_back(jnp.transpose(dk[part, :], (1, 0)), ktab_ref[i, :half], ktab_ref[i, half:])
            dkv_ref[i, base : base + size, :] = back.astype(BF16)
            dkv_ref[i, base + size : base + 2 * size, :] = jnp.transpose(dv[part, :], (1, 0)).astype(BF16)


def attend_back(part, pos, q, o, do, lse, kv, qtab, ktab, bq, bk, sub, span):
    nq, blocks = pos.shape[1], pos.shape[1] // sub
    nk = blocks * span
    groups, size, rows = GROUP, HEAD_SIZE, QROWS
    tile = pl.BlockSpec((bq // sub, rows, sub), lambda i: (i, 0, 0))
    if sub == span == bq:
        out_specs = [whole(blocks, SLICE, span)]
        out_shape = [jax.ShapeDtypeStruct((blocks, SLICE, span), BF16)]
    else:
        out_specs = [tile, whole(blocks, 2 * size, span)]
        out_shape = [
            jax.ShapeDtypeStruct((blocks, rows, sub), BF16),
            jax.ShapeDtypeStruct((blocks, 2 * size, span), BF16),
        ]
    return pl.pallas_call(
        functools.partial(attend_back_kernel, bk, sub, span),
        grid=(nq // bq,),
        in_specs=[
            pl.BlockSpec(memory_space=pltpu.SMEM),
            pl.BlockSpec((1, bq), lambda i: (0, i)),
            tile,
            tile,
            tile,
            pl.BlockSpec((groups, 1, bq), lambda i: (0, 0, i)),
            whole(blocks, 2 * size, span),
            pl.BlockSpec((bq // sub, size, sub), lambda i: (i, 0, 0)),
            whole(blocks, size, span),
        ],
        out_specs=out_specs,
        out_shape=out_shape,
        scratch_shapes=[
            pltpu.VMEM((groups, size, bq), BF16),
            pltpu.VMEM((nk, size), BF16),
            pltpu.VMEM((size, nk), BF16),
            pltpu.VMEM((nk, size), BF16),
            pltpu.VMEM((groups, bq, size), BF16),
            pltpu.VMEM((groups, size, bq), BF16),
            pltpu.VMEM((groups, bq, size), BF16),
            pltpu.VMEM((groups, 1, bq), F32),
            pltpu.VMEM((groups, size, bq), F32),
            pltpu.VMEM((nk, size), F32),
            pltpu.VMEM((nk, size), F32),
        ],
        compiler_params=params("arbitrary"),
        cost_estimate=COST,
        name="attend_back",
    )(part, pos, q, o, do, lse, kv, qtab, ktab)


def chosen_rows(rank, cap):
    return lax.broadcasted_iota(jnp.int32, (cap, rank.shape[1]), 0) == rank


def dispatch_kernel(cap, rank_ref, token_ref, row_ref):
    for e in range(rank_ref.shape[0]):
        one = chosen_rows(rank_ref[e], cap).astype(F32).astype(BF16)
        row_ref[e] = jnp.dot(one, token_ref[...], preferred_element_type=F32).astype(BF16)


def dispatch(rank, tokens, block, cap, wide):
    count = rank.shape[0]
    span, width = tokens.shape
    return pl.pallas_call(
        functools.partial(dispatch_kernel, cap),
        grid=(width // wide,),
        in_specs=[
            pl.BlockSpec((count, 1, span), lambda i: (0, 0, block)),
            pl.BlockSpec((span, wide), lambda i: (0, i)),
        ],
        out_specs=pl.BlockSpec((count, cap, wide), lambda i: (0, 0, i)),
        out_shape=jax.ShapeDtypeStruct((count, cap, width), BF16),
        compiler_params=params("arbitrary"),
        cost_estimate=COST,
        name="dispatch",
    )(rank, tokens)


def experts_kernel(span, cap, offset, blocks, place_ref, rank_ref, prob_ref, *refs):
    x_refs, g_refs = refs[:blocks], refs[blocks : 2 * blocks]
    gu_ref, dn_ref, back_ref, out_ref, mine_ref, theirs_ref, grads = refs[2 * blocks :]
    e = pl.program_id(0)
    x = jnp.concatenate([ref[0] for ref in x_refs], axis=0)
    g = jnp.concatenate([ref[0] for ref in g_refs], axis=0)
    width = x.shape[1]
    ps = []
    for i in range(blocks):
        rows = slice(i * span, (i + 1) * span)
        hit = chosen_rows(rank_ref[0, :, rows], cap)
        ps.append(jnp.sum(jnp.where(hit, prob_ref[0, :, rows], 0.0), axis=1, keepdims=True))
    prob = jnp.concatenate(ps, axis=0)
    mixed = jnp.dot(x, gu_ref[0], preferred_element_type=F32)
    gate, up = mixed[:, :FFE], mixed[:, FFE:]
    logistic = 1.0 / (1.0 + jnp.exp(-gate))
    act = (gate * logistic * up).astype(BF16)
    sent = (prob * g.astype(F32)).astype(BF16)
    act_grad = contract(sent, dn_ref[0], 1, 1)
    mix = jnp.concatenate(
        [act_grad * up * logistic * (1.0 + gate * (1.0 - logistic)), act_grad * gate * logistic], axis=1
    ).astype(BF16)
    out = jnp.dot(act, dn_ref[0], preferred_element_type=F32).astype(BF16).astype(F32)
    route = jnp.sum(g.astype(F32) * out, axis=1, keepdims=True)
    out_ref[0] = (prob * out).astype(BF16)
    back_ref[0, :, :width] = contract(mix, gu_ref[0], 1, 1).astype(BF16)
    high = route.astype(BF16).astype(F32)
    place = lax.broadcasted_iota(jnp.int32, (route.shape[0], EXTRA), 1) - (place_ref[0] + offset + e)
    extra = jnp.where(place == 0, high, jnp.where(place == EXPERTS, route - high, 0.0))
    back_ref[0, :, width:] = extra.astype(BF16)
    grads[:, : 2 * FFE] = contract(x, mix, 0, 0).astype(BF16)
    grads[:, 2 * FFE :] = contract(sent, act, 0, 0).astype(BF16)
    pairs, _, own, _ = mine_ref.shape
    core = place_ref[1]
    for i in range(pairs):
        mine_ref[i, 0] = grads[pl.ds(pl.multiple_of((2 * i + core) * own, own), own), :]
        theirs_ref[i, 0] = grads[pl.ds(pl.multiple_of((2 * i + 1 - core) * own, own), own), :]


def run_experts(place, rank, prob, xs, gs, gateup, down, offset, count, n_ctx, span, cap):
    blocks = len(xs)
    width = gateup.shape[1]
    rows = blocks * cap
    tokens = blocks * span
    own = width // n_ctx
    pairs = n_ctx // 2

    def picked(*shape):
        return pl.BlockSpec((1,) + shape, lambda e: (e + offset, 0, 0))

    def row(wide):
        return pl.BlockSpec((1, rows, wide), lambda e: (e, 0, 0))

    half = pl.BlockSpec((pairs, 1, own, 3 * FFE), lambda e: (0, e, 0, 0))
    half_shape = jax.ShapeDtypeStruct((pairs, count, own, 3 * FFE), BF16)
    return pl.pallas_call(
        functools.partial(experts_kernel, span, cap, offset, blocks),
        grid=(count,),
        in_specs=[pl.BlockSpec(memory_space=pltpu.SMEM), picked(1, tokens), picked(1, tokens)]
        + [picked(cap, width)] * (2 * blocks)
        + [picked(width, 2 * FFE), picked(FFE, width)],
        out_specs=[row(width + EXTRA), row(width), half, half],
        out_shape=[
            jax.ShapeDtypeStruct((count, rows, width + EXTRA), BF16),
            jax.ShapeDtypeStruct((count, rows, width), BF16),
            half_shape,
            half_shape,
        ],
        scratch_shapes=[pltpu.VMEM((width, 3 * FFE), BF16)],
        compiler_params=params("arbitrary"),
        cost_estimate=pl.CostEstimate(
            flops=2 * count * rows * width * 9 * FFE, bytes_accessed=count * rows * width * 8, transcendentals=0
        ),
        name="experts",
    )(place, rank, prob, *xs, *gs, gateup, down)


def add_kernel(left_ref, right_ref, sum_ref):
    sum_ref[...] = (left_ref[...].astype(F32) + right_ref[...].astype(F32)).astype(BF16)


def add(left, right):
    pairs, count, own, wide = left.shape
    block = pl.BlockSpec((1, 1, own, wide), lambda i, e: (i, e, 0, 0))
    return pl.pallas_call(
        add_kernel,
        grid=(pairs, count),
        in_specs=[block, block],
        out_specs=block,
        out_shape=jax.ShapeDtypeStruct(left.shape, BF16),
        compiler_params=params("arbitrary", "arbitrary"),
        cost_estimate=COST,
        name="add",
    )(left, right)


def outer_kernel(rows_ref, grad_ref, side_ref, full_ref):
    owners, _, piece, _ = full_ref.shape
    width = grad_ref.shape[1]
    product = jnp.dot(rows_ref[...], grad_ref[...], preferred_element_type=F32).astype(BF16)
    for i in range(owners):
        part = slice(i * piece, (i + 1) * piece)
        full_ref[i, 0, :, :width] = product[part]
        full_ref[i, 0, :, width:] = side_ref[part, :]


def outer(rows, grad, side, owners, own):
    height, span = rows.shape
    width = grad.shape[1]
    wide = width + side.shape[1]
    return pl.pallas_call(
        outer_kernel,
        grid=(height // own,),
        in_specs=[
            pl.BlockSpec((own, span), lambda c: (c, 0)),
            whole(span, width),
            pl.BlockSpec((own, side.shape[1]), lambda c: (c, 0)),
        ],
        out_specs=pl.BlockSpec((owners, 1, own // owners, wide), lambda c: (0, c, 0, 0)),
        out_shape=jax.ShapeDtypeStruct((owners, height // own, own // owners, wide), BF16),
        compiler_params=params("arbitrary"),
        cost_estimate=COST,
        name="outer",
    )(rows, grad, side)


def gather_parts_kernel(mixed_ref, head_ref, part_ref):
    count, _, wide = mixed_ref.shape
    part_ref[:, :wide] = sum(mixed_ref[c].astype(F32) for c in range(count)).astype(BF16)
    for h in range(KEY_VALUE_HEADS):
        head = head_ref[h]
        part_ref[:, wide + h * QROWS : wide + (h + 1) * QROWS] = head[:, :QROWS]
        base = wide + KEY_VALUE_HEADS * QROWS
        for i in range(2):
            start = base + (i * KEY_VALUE_HEADS + h) * HEAD_SIZE
            part_ref[:, start : start + HEAD_SIZE] = head[:, QROWS + i * HEAD_SIZE : QROWS + (i + 1) * HEAD_SIZE]


def gather_parts(mixed, heads):
    _, piece, wide = mixed.shape
    total = wide + KEY_VALUE_HEADS * SLICE
    return pl.pallas_call(
        gather_parts_kernel,
        grid=(1,),
        in_specs=[whole(*mixed.shape), whole(*heads.shape)],
        out_specs=whole(piece, total),
        out_shape=jax.ShapeDtypeStruct((piece, total), BF16),
        compiler_params=params("arbitrary"),
        cost_estimate=COST,
        name="gather_parts",
    )(mixed, heads)


def finish_kernel(count, me_ref, *refs):
    blocks, (wq, wk, wv, q_ref, k_ref, v_ref, o_ref, side_ref) = refs[:count], refs[count:]
    piece = blocks[0].shape[0]
    width, heads, pair = q_ref.shape[1], k_ref.shape[1], EXPERTS + 1
    for i in range(count):
        rows = pl.ds(pl.multiple_of((me_ref[0] ^ i) * piece, piece), piece)
        block = blocks[i][...].astype(F32)
        o_ref[rows, :] = block[:, :width]
        start = width + EXTRA
        query, key = block[:, start : start + width], block[:, start + width : start + width + heads]
        value = block[:, start + width + heads :]
        q_ref[rows, :], k_ref[rows, :], v_ref[rows, :] = query, key, value
        inner = jnp.sum(wq[rows, :].astype(F32) * query, axis=1, keepdims=True)
        inner += jnp.sum(wk[rows, :].astype(F32) * key, axis=1, keepdims=True)
        inner += jnp.sum(wv[rows, :].astype(F32) * value, axis=1, keepdims=True)
        column = lax.broadcasted_iota(jnp.int32, (piece, EXTRA), 1)
        side_ref[rows, :] = jnp.where(column == pair, inner, block[:, width:start])


def finish(me, blocks, query_weight, key_matrix, value_matrix):
    weights = [query_weight, key_matrix, value_matrix]
    own, width = query_weight.shape
    shapes = [array.shape for array in weights] + [(own, width), (own, EXTRA)]
    return pl.pallas_call(
        functools.partial(finish_kernel, len(blocks)),
        grid=(1,),
        in_specs=[pl.BlockSpec(memory_space=pltpu.SMEM)] + [whole(*array.shape) for array in [*blocks, *weights]],
        out_specs=[whole(*shape) for shape in shapes],
        out_shape=[jax.ShapeDtypeStruct(shape, F32) for shape in shapes],
        compiler_params=params("arbitrary"),
        cost_estimate=COST,
        name="finish",
    )(me.astype(jnp.int32).reshape(1), *blocks, *weights)


def unpack_kernel(sum_ref, *refs):
    gateup_ref, down_ref = refs[-2:]
    gateup_ref[0] = sum_ref[0, :, : 2 * FFE].astype(F32)
    down_ref[0] = sum_ref[0, :, 2 * FFE :].astype(F32)


def unpack(total, offset, experts, held):
    count, own, wide = total.shape
    return pl.pallas_call(
        unpack_kernel,
        grid=(count,),
        in_specs=[pl.BlockSpec((1, own, wide), lambda e: (e, 0, 0))] + [pl.BlockSpec(memory_space=pl.ANY)] * len(held),
        out_specs=[
            pl.BlockSpec((1, own, 2 * FFE), lambda e: (e + offset, 0, 0)),
            pl.BlockSpec((1, own, FFE), lambda e: (e + offset, 0, 0)),
        ],
        out_shape=[
            jax.ShapeDtypeStruct((experts, own, 2 * FFE), F32),
            jax.ShapeDtypeStruct((experts, own, FFE), F32),
        ],
        input_output_aliases={1 + i: i for i in range(len(held))},
        compiler_params=params("arbitrary"),
        cost_estimate=COST,
        name="unpack",
    )(total, *held)


def combine_kernel(cap, n_parts, *refs):
    rank_refs, row_refs, out_ref = refs[:n_parts], refs[n_parts : 2 * n_parts], refs[-1]
    total = None
    for rank_ref, row_ref in zip(rank_refs, row_refs):
        ones, rows = [], []
        for e in range(rank_ref.shape[0]):
            ones.append(chosen_rows(rank_ref[e], cap).astype(F32).astype(BF16))
            rows.append(row_ref[e])
        part = contract(jnp.concatenate(ones, axis=0), jnp.concatenate(rows, axis=0), 0, 0)
        total = part if total is None else total + part
    out_ref[...] = total.astype(BF16)


def combine(ranks, rows, block, span, cap, wide):
    width = rows[0].shape[2]
    count = sum(r.shape[0] for r in ranks)
    return pl.pallas_call(
        functools.partial(combine_kernel, cap, len(ranks)),
        grid=(width // wide,),
        in_specs=[pl.BlockSpec((r.shape[0], 1, span), lambda i: (0, 0, block)) for r in ranks]
        + [pl.BlockSpec((r.shape[0], cap, wide), lambda i: (0, block, i)) for r in rows],
        out_specs=pl.BlockSpec((span, wide), lambda i: (0, i)),
        out_shape=jax.ShapeDtypeStruct((span, width), BF16),
        compiler_params=params("arbitrary"),
        cost_estimate=COST,
        name="combine",
    )(*ranks, *rows)


def swapped(array, axis, mask):
    count = lax.axis_size(axis)
    return lax.ppermute(array, axis, [(i, i ^ mask) for i in range(count)])


def gather_blocks(array, axis):
    count = lax.axis_size(axis)
    if count != 4:
        return [array] + [swapped(array, axis, k) for k in range(1, count)]
    half = array.shape[0] // 2
    one, two = swapped(array, axis, 1), swapped(array, axis, 2)
    far = jnp.concatenate([swapped(two[:half], axis, 1), swapped(one[half:], axis, 2)], axis=0)
    return [array, one, two, far]


def gather_start(array, axis):
    return [array, swapped(array, axis, 1), swapped(array, axis, 2)]


def gather_end(array, one, two, axis):
    count = lax.axis_size(axis)
    if count != 4:
        return [array, one, two] + [swapped(array, axis, k) for k in range(3, count)]
    half = array.shape[0] // 2
    far = jnp.concatenate([swapped(two[:half], axis, 1), swapped(one[half:], axis, 2)], axis=0)
    return [array, one, two, far]


def gather_rows(array, axis, use, early):
    count = lax.axis_size(axis)
    if count != 4:
        return [use(block, k) for k, block in enumerate(gather_blocks(array, axis))], early
    half = array.shape[0] // 2
    one, two = swapped(array, axis, 1), swapped(array, axis, 2)
    own = use(array, 0)
    own, one, two, early = lax.optimization_barrier((own, one, two, early))
    far = jnp.concatenate([swapped(two[:half], axis, 1), swapped(one[half:], axis, 2)], axis=0)
    one, two, far = lax.optimization_barrier((use(one, 1), use(two, 2), far))
    return [own, one, two, use(far, 3)], early


def wide_sum(*arrays):
    return sum(array.astype(F32) for array in arrays)


def return_start(parts, axis):
    if lax.axis_size(axis) != 4:
        return [parts[0]] + [swapped(parts[k], axis, k) for k in range(1, len(parts))]
    own, one, two, far = parts
    half = own.shape[0] // 2
    via_one, via_two = swapped(far[:half], axis, 1), swapped(far[half:], axis, 2)
    return [own, one, two, via_one, via_two, swapped(one[:half], axis, 1), swapped(two[half:], axis, 2)]


def return_end(held, axis):
    if lax.axis_size(axis) != 4:
        return wide_sum(*held)
    own, one, two, via_one, via_two, one_low, two_high = held
    half = own.shape[0] // 2
    one_high = swapped(wide_sum(one[half:], via_two).astype(BF16), axis, 1)
    two_low = swapped(wide_sum(two[:half], via_one).astype(BF16), axis, 2)
    return jnp.concatenate(
        [wide_sum(own[:half], one_low, two_low), wide_sum(own[half:], one_high, two_high)], axis=0
    )


def for_partners(array, axis, dim):
    count, me = lax.axis_size(axis), lax.axis_index(axis)
    return [lax.dynamic_index_in_dim(array, me ^ k, dim, keepdims=False) for k in range(count)]


def sum_from_partners(parts, axis):
    return wide_sum(parts[0], *[swapped(parts[k], axis, k) for k in range(1, len(parts))]).astype(BF16)


def in_order(blocks, axis):
    me = lax.axis_index(axis)
    blocks = jnp.stack(blocks)
    return jnp.stack([lax.dynamic_index_in_dim(blocks, me ^ k, 0, keepdims=False) for k in range(blocks.shape[0])])


def all_of_expert(array):
    count = lax.axis_size("expert")
    return in_order([array] + [swapped(array, "expert", k) for k in range(1, count)], "expert")


def norm_rows(values, gain):
    factor = lax.rsqrt(jnp.mean(values * values, axis=-1, keepdims=True) + EPS)
    return (values * factor * gain).astype(BF16), factor


def norm_back(grad_norm, values, factor, gain):
    inner = grad_norm * gain
    return factor * inner - values * factor**3 * jnp.mean(inner * values, axis=-1, keepdims=True)


def angles(positions):
    half = HEAD_SIZE // 2
    freq = jnp.power(THETA, -jnp.arange(half).astype(F32) / half)
    turned = freq[None, :, None] * positions.astype(F32)[:, None, :]
    return jnp.concatenate([jnp.cos(turned), jnp.sin(turned)], axis=1)


def per_device(
    inputs,
    cotangent,
    routes,
    attn_gain,
    query_weight,
    key_matrix,
    value_matrix,
    output_matrix,
    ffn_gain,
    router_weight,
    gateup_weight,
    down_weight,
):
    _, span, width = inputs.shape
    n_ctx = lax.axis_size("ctx")
    n_owner = lax.axis_size("expert")
    own_rows = query_weight.shape[0]
    local_experts = gateup_weight.shape[0]
    cap = span // 4
    parts = n_ctx // KEY_VALUE_HEADS
    sub = span // parts
    part = lax.axis_index("ctx") % parts
    part_arg = part.astype(jnp.int32).reshape(1)

    tokens_in = inputs.reshape(span, width)
    me = lax.axis_index("expert")
    piece = own_rows // n_owner

    def a_part(array):
        return lax.dynamic_slice_in_dim(array, me * piece, piece, 0)

    heads = jnp.concatenate(
        [
            a_part(query_weight).reshape(piece, KEY_VALUE_HEADS, QROWS),
            a_part(key_matrix).reshape(piece, KEY_VALUE_HEADS, HEAD_SIZE),
            a_part(value_matrix).reshape(piece, KEY_VALUE_HEADS, HEAD_SIZE),
        ],
        axis=-1,
    ).transpose(1, 0, 2)
    small = jnp.concatenate([attn_gain[:, None], ffn_gain[:, None], router_weight], axis=1)
    small = a_part(jnp.pad(small, ((0, 0), (0, HEAD_SIZE - small.shape[1]))))
    sends = jnp.concatenate(
        [jnp.repeat(heads, parts, axis=0), jnp.broadcast_to(small[None], (n_ctx,) + small.shape)], axis=-1
    )
    weights = all_of_expert(lax.all_to_all(sends, "ctx", 0, 0, tiled=True))
    weights = weights.transpose(1, 0, 2, 3).reshape(width, -1)
    head_weight = weights[:, :SLICE].T
    gain_one = weights[:, SLICE].astype(F32)
    gain_two = weights[:, SLICE + 1].astype(F32)
    router = weights[:, SLICE + 2 : SLICE + 2 + EXPERTS]

    names = routes.reshape(span, TOPK)
    hits = jnp.any(names[:, :, None] == jnp.arange(EXPERTS), axis=1)
    upto = (jnp.arange(span)[:, None] <= jnp.arange(span)[None, :]).astype(BF16)
    counted = contract(hits.astype(BF16), upto, 0, 0)
    ranks = jnp.where(hits.T, counted - 1.0, -1.0).astype(BF16)

    def to_owners(array):
        array = lax.all_to_all(array.reshape(n_owner, local_experts, span), "expert", 0, 0, tiled=True)
        blocks = [lax.dynamic_index_in_dim(array, me ^ k, 0, keepdims=False) for k in range(n_owner)]
        return jnp.concatenate(blocks, axis=1)[:, None]

    every = jnp.arange(n_ctx * span, dtype=jnp.int32).reshape(n_ctx, span)
    table = angles(every)
    cut = span * 3 // 4 if span % 512 == 0 else span // 2
    x_pieces = [
        lax.all_gather(part_in, "ctx", axis=0, tiled=False) for part_in in (tokens_in[:cut], tokens_in[cut:])
    ]
    grad_in = cotangent.reshape(span, width)
    held = gather_start(grad_in, "expert")
    rank = to_owners(ranks)
    x_pieces[0], held, head_weight, rank = lax.optimization_barrier((x_pieces[0], held, head_weight, rank))
    rank = rank.astype(jnp.int32)
    grad_blocks = gather_end(*held, "expert")
    buffers = project(x_pieces[0], gain_one[None], head_weight, table, 0, ())
    x_pieces[1], grad_blocks, buffers = lax.optimization_barrier((x_pieces[1], grad_blocks, buffers))
    normed_all, q_all, kv_all = project(x_pieces[1], gain_one[None], head_weight, table, cut // (span - cut), buffers)
    if parts == 1:
        queries, positions, q_table = q_all, every, table
    else:

        def mine(array):
            array = array.reshape(array.shape[:-1] + (parts, sub))
            return lax.dynamic_index_in_dim(array, part, array.ndim - 2, keepdims=False)

        queries, positions, q_table = mine(q_all), mine(every), mine(table)
    pos = positions.reshape(1, -1)

    output_matrix, w_heads, queries = lax.optimization_barrier((output_matrix, head_weight, queries))
    w_output = lax.all_gather(output_matrix, "ctx", axis=0, tiled=True)
    grad_rows = [dispatch(rank, block, k, cap, width // 2) for k, block in enumerate(grad_blocks)]
    tile = min(512, n_ctx * sub)
    attended, lse = attend(part_arg, pos, queries, kv_all, tile, tile, sub, span)

    def to_rows(array):
        array = lax.all_to_all(array, "ctx", 0, 0, tiled=True)
        array = array.reshape(KEY_VALUE_HEADS, parts, -1, sub).transpose(0, 2, 1, 3)
        return array.reshape(-1, span)

    attended_rows, grad_rows = lax.optimization_barrier((to_rows(attended), grad_rows))
    flat_in = tokens_in.astype(F32)
    hidden = flat_in + contract(attended_rows, w_output, 0, 0)
    normed_two, rms_two = norm_rows(hidden, gain_two)
    w_heads, normed_two = lax.optimization_barrier((w_heads, normed_two))
    w_heads = lax.all_gather(w_heads, "ctx", axis=0, tiled=False)[::parts].reshape(-1, width)
    logits = jnp.dot(normed_two, router, preferred_element_type=F32)
    masked = jnp.where(hits, logits, NEG)
    powers = jnp.where(hits, jnp.exp(masked - jnp.max(masked, axis=-1, keepdims=True)), 0.0)
    probs = powers / jnp.sum(powers, axis=-1, keepdims=True)
    prob = to_owners(probs.T)

    place = jnp.stack([me * local_experts, lax.axis_index("ctx") % 2]).astype(jnp.int32)
    token_rows, prob = gather_rows(
        normed_two, "expert", lambda block, k: dispatch(rank, block, k, cap, width // 2), prob
    )
    cuts, offset = [], 0
    for count in (1, 1, 3, 3, local_experts):
        if offset < local_experts:
            cuts.append((offset, min(count, local_experts - offset)))
            offset += count
    backs, outs, sums = [], [], []
    core_line = [[z * 2 + core for z in range(n_ctx // 2)] for core in range(2)]

    def line_sum(pair):
        total = lax.psum_scatter(
            pair.reshape(-1, 3 * FFE), "ctx", scatter_dimension=0, tiled=True, axis_index_groups=core_line
        )
        return total.reshape(-1, own_rows, 3 * FFE)

    pairs, pair_sums = [], []
    for number, (offset, count) in enumerate(cuts):
        if number == 1:
            w_heads, place, _ = lax.optimization_barrier((w_heads, place, backs[0]))
        elif number > 1:
            if number > 2:
                pairs[number - 2], _ = lax.optimization_barrier((pairs[number - 2], backs[-1]))
            pair_sums.append(add(*pairs[number - 2]))
            place, _, _ = lax.optimization_barrier((place, backs[-1], pair_sums[-1]))
        back, out, mine, theirs = run_experts(
            place, rank, prob, token_rows, grad_rows, gateup_weight, down_weight, offset, count, n_ctx, span, cap
        )
        backs.append(back)
        outs.append(out)
        pairs.append((mine, swapped(theirs, "ctx", 1)))
        if number > 1:
            sums.append(line_sum(pair_sums[-1]))
    ranks = [rank[offset : offset + count] for offset, count in cuts]

    def to_tokens(rows):
        return [combine(ranks, rows, k, span, cap, rows[0].shape[2]) for k in reversed(range(n_owner))][::-1]

    back_sum = return_end(return_start(to_tokens(backs), "expert"), "expert")

    grad = cotangent.reshape(span, width).astype(F32)
    route_grad = back_sum[:, width : width + EXPERTS] + back_sum[:, width + EXPERTS : width + 2 * EXPERTS]
    chosen_grad = probs * (route_grad - jnp.sum(probs * route_grad, axis=-1, keepdims=True))
    logit_grad = chosen_grad.astype(BF16)
    normed_two_grad = back_sum[:, :width] + contract(logit_grad, router, 1, 1)
    ffn_gain_full = jnp.sum(normed_two_grad * hidden * rms_two, axis=0)
    hidden_grad = grad + norm_back(normed_two_grad, hidden, rms_two, gain_two)
    hidden_low = hidden_grad.astype(BF16)
    attended_grad = contract(w_output, hidden_low, 1, 1).astype(BF16)
    attended_grad, hidden_low, logit_grad, pairs = lax.optimization_barrier(
        (attended_grad, hidden_low, logit_grad, pairs[-2:])
    )
    sums.append(line_sum(add(*pairs[0])))
    router_full = contract(normed_two, logit_grad, 0, 0)
    attended_grad = attended_grad.reshape(KEY_VALUE_HEADS, QROWS, parts, sub).transpose(0, 2, 1, 3)
    attended_grad = lax.all_to_all(attended_grad.reshape(n_ctx, QROWS, sub), "ctx", 0, 0, tiled=True)
    column = jnp.arange(EXTRA)[None]
    side = jnp.where(
        column == EXPERTS, ffn_gain_full[:, None], jnp.pad(router_full, ((0, 0), (0, EXTRA - EXPERTS)))
    ).astype(BF16)
    mixed_parts = for_partners(outer(attended_rows, hidden_low, side, n_owner, own_rows), "expert", 0)
    earlier = sums[:-1]
    pairs[1], outs, earlier, mixed_parts = lax.optimization_barrier((pairs[1], outs, earlier, mixed_parts))
    pair = add(*pairs[1])
    grads = ()
    for (offset, _), total in zip(cuts, earlier):
        grads = unpack(total, offset, local_experts, grads)
    out_parts, attended_grad, grads, mixed_part, pair = lax.optimization_barrier(
        (to_tokens(outs), attended_grad, grads, sum_from_partners(mixed_parts, "expert"), pair)
    )
    mixed_part = lax.all_to_all(mixed_part, "ctx", 0, 0, tiled=True)
    backs = attend_back(
        part_arg, pos, queries, attended, attended_grad, lse, kv_all, q_table, table, tile, tile, sub, span
    )
    mixed_part, backs = lax.optimization_barrier((mixed_part, backs))
    if len(backs) == 1:
        rows_back = lax.all_to_all(backs[0], "ctx", 0, 0, tiled=True).reshape(-1, span)
        head_grad = head_grads(backs[0], normed_all)
    else:
        query_back, kv_back = backs
        query_rows = to_rows(query_back).reshape(KEY_VALUE_HEADS, QROWS, span)
        kv_rows = lax.all_to_all(kv_back, "ctx", 0, 0, tiled=True).astype(F32)
        kv_rows = jnp.sum(kv_rows.reshape(KEY_VALUE_HEADS, parts, 2 * HEAD_SIZE, span), axis=1).astype(BF16)
        rows_back = jnp.concatenate([query_rows, kv_rows], axis=1).reshape(-1, span)
        normed_part = normed_all.reshape(n_ctx, parts, sub, width)
        normed_part = lax.dynamic_index_in_dim(normed_part, part, 1, keepdims=False)
        head_grad = jnp.concatenate([head_grads(query_back, normed_part), head_grads(kv_back, normed_all)], axis=1)
    head_parts = for_partners(head_grad.reshape(n_ctx, n_owner, -1, SLICE), "expert", 1)
    head_part = sum_from_partners(head_parts, "expert")
    grads = unpack(sums[-1], cuts[-2][0], local_experts, grads)
    pair, rows_back, head_part = lax.optimization_barrier((pair, rows_back, head_part))
    head_part, out_parts = lax.optimization_barrier((head_part, out_parts))
    head_part = lax.all_to_all(head_part, "ctx", 0, 0, tiled=True)
    output = hidden + return_end(return_start(out_parts, "expert"), "expert")
    output = output.astype(BF16).reshape(1, span, width)
    sums.append(line_sum(pair))
    gateup_grad, down_grad = unpack(sums[-1], cuts[-1][0], local_experts, grads)
    down_grad = down_grad.transpose(0, 2, 1)
    if parts > 1:
        head_part = jnp.sum(head_part.astype(F32).reshape(KEY_VALUE_HEADS, parts, piece, SLICE), axis=1).astype(BF16)
    summed = gather_parts(mixed_part, head_part)
    summed = [summed] + [swapped(summed, "expert", k) for k in range(1, n_owner)]
    place = me
    if piece % 16:
        summed, place = [in_order(summed, "expert").reshape(own_rows, -1)], 0 * me
    query_grad, key_grad, value_grad, outproj_grad, side = finish(
        place, summed, query_weight, key_matrix, value_matrix
    )
    router_grad, ffn_gain_grad = side[:, :EXPERTS], side[:, EXPERTS]
    attn_gain_grad = side[:, EXPERTS + 1] / attn_gain.astype(F32)
    normed_one_grad = contract(rows_back, w_heads, 0, 0)
    rms_one = lax.rsqrt(jnp.mean(flat_in * flat_in, axis=-1, keepdims=True) + EPS)
    input_grad = (
        (hidden_grad + norm_back(normed_one_grad, flat_in, rms_one, gain_one)).astype(BF16).reshape(1, span, width)
    )
    return (
        output,
        input_grad,
        attn_gain_grad,
        query_grad,
        key_grad,
        value_grad,
        outproj_grad,
        ffn_gain_grad,
        router_grad,
        gateup_grad,
        down_grad,
    )


def solution(mesh):
    tokens = P("expert", "ctx", None)
    row = P("ctx")
    rows = P("ctx", None)
    owned = P("expert", None, None)
    return jax.shard_map(
        per_device,
        mesh=mesh,
        in_specs=(tokens, tokens, tokens, row, rows, rows, rows, rows, row, rows, owned, owned),
        out_specs=(
            tokens,
            tokens,
            row,
            rows,
            rows,
            rows,
            rows,
            row,
            rows,
            P("expert", "ctx", None),
            P("expert", None, "ctx"),
        ),
        check_vma=False,
    )
```

```python
import functools

import jax
import jax.numpy as jnp
from jax import lax
from jax.experimental import pallas as pl
from jax.experimental.pallas import tpu as pltpu
from jax.sharding import PartitionSpec as P

QUERY_HEADS = 24
KEY_VALUE_HEADS = 8
HEAD_SIZE = 64
GROUP = QUERY_HEADS // KEY_VALUE_HEADS
QROWS = GROUP * HEAD_SIZE
SLICE = QROWS + 2 * HEAD_SIZE
FFE = 512
EXPERTS = 40
TOPK = 8
EXTRA = 128

EPS = 1e-05
NEG = -1e30
THETA = 10000.0
LOG2_E = 1.4426950408889634

F32 = jnp.float32
BF16 = jnp.bfloat16
VMEM_LIMIT = 60 * 1024 * 1024
COST = pl.CostEstimate(flops=1024, bytes_accessed=1024, transcendentals=0)


def contract(left, right, a, b):
    return lax.dot_general(left, right, (((a,), (b,)), ((), ())), preferred_element_type=F32)


def params(*order):
    return pltpu.CompilerParams(vmem_limit_bytes=VMEM_LIMIT, dimension_semantics=order)


def whole(*shape):
    return pl.BlockSpec(shape, lambda *_: (0,) * len(shape))


def project_kernel(x_ref, gain_ref, w_ref, table_ref, *refs):
    n_ref, q_ref, kv_ref = refs[-3:]
    half = HEAD_SIZE // 2
    x = x_ref[0].astype(F32)
    factor = lax.rsqrt(jnp.mean(x * x, axis=-1, keepdims=True) + EPS)
    normed = (x * factor * gain_ref[...]).astype(BF16)
    n_ref[0] = normed
    raw = contract(w_ref[...], normed, 1, 1)
    cosine, sine = table_ref[0, :half], table_ref[0, half:]
    scale = HEAD_SIZE**-0.5 * LOG2_E
    for g in range(GROUP + 1):
        a, b = raw[g * HEAD_SIZE : g * HEAD_SIZE + half], raw[g * HEAD_SIZE + half : (g + 1) * HEAD_SIZE]
        turned = jnp.concatenate([a * cosine - b * sine, b * cosine + a * sine], axis=0)
        if g < GROUP:
            q_ref[0, g * HEAD_SIZE : (g + 1) * HEAD_SIZE, :] = (turned * scale).astype(BF16)
        else:
            kv_ref[0, :HEAD_SIZE, :] = turned.astype(BF16)
    kv_ref[0, HEAD_SIZE:, :] = raw[QROWS + HEAD_SIZE :].astype(BF16)


def project(x, gain, w_rows, table, which, held):
    blocks, columns, width = x.shape
    span = table.shape[2]
    shapes = [(blocks, span, width), (blocks, QROWS, span), (blocks, 2 * HEAD_SIZE, span)]
    return pl.pallas_call(
        project_kernel,
        grid=(blocks,),
        in_specs=[
            pl.BlockSpec((1, columns, width), lambda b: (b, 0, 0)),
            whole(1, width),
            whole(SLICE, width),
            pl.BlockSpec((1, HEAD_SIZE, columns), lambda b: (b, 0, which)),
        ]
        + [pl.BlockSpec(memory_space=pl.ANY)] * len(held),
        out_specs=[
            pl.BlockSpec((1, columns, width), lambda b: (b, which, 0)),
            pl.BlockSpec((1, QROWS, columns), lambda b: (b, 0, which)),
            pl.BlockSpec((1, 2 * HEAD_SIZE, columns), lambda b: (b, 0, which)),
        ],
        out_shape=[jax.ShapeDtypeStruct(shape, BF16) for shape in shapes],
        input_output_aliases={4 + i: i for i in range(len(held))},
        compiler_params=params("arbitrary"),
        cost_estimate=COST,
        name="project",
    )(x, gain, w_rows, table, *held)


def head_grads_kernel(back_ref, n_ref, grad_ref, acc):
    b = pl.program_id(0)
    part = contract(n_ref[0], back_ref[0], 0, 1)

    @pl.when(b == 0)
    def _():
        acc[...] = part

    @pl.when(b > 0)
    def _():
        acc[...] += part

    @pl.when(b == pl.num_programs(0) - 1)
    def _():
        grad_ref[...] = acc[...].astype(BF16)


def head_grads(back, normed):
    blocks, rows, span = back.shape
    width = normed.shape[2]
    return pl.pallas_call(
        head_grads_kernel,
        grid=(blocks,),
        in_specs=[
            pl.BlockSpec((1, rows, span), lambda b: (b, 0, 0)),
            pl.BlockSpec((1, span, width), lambda b: (b, 0, 0)),
        ],
        out_specs=whole(width, rows),
        out_shape=jax.ShapeDtypeStruct((width, rows), BF16),
        scratch_shapes=[pltpu.VMEM((width, rows), F32)],
        compiler_params=params("arbitrary"),
        cost_estimate=COST,
        name="head_grads",
    )(back, normed)


def key_tiles(first, count, sub, span, part, bk):
    low = (first // sub) * span + part * sub + first % sub
    last = first + count - 1
    high = (last // sub) * span + part * sub + last % sub
    return (low + 1) // bk, (high + bk) // bk


def tile_parts(bk, bq, sub, span, masked):
    if masked and bk == bq == sub == span:
        half = bk // 2
        return [(0, half, slice(0, bq)), (half, half, slice(half, bq))]
    return [(0, bk, slice(0, bq))]


def loop(first, last, step):
    def body(j, carry):
        step(j)
        return carry

    lax.fori_loop(first, last, body, 0)


def unpack_blocks(refs, out):
    groups, size, _ = out.shape
    for i in range(refs.shape[0]):
        columns = refs.shape[2]
        for g in range(groups):
            out[g, :, i * columns : (i + 1) * columns] = refs[i, g * size : (g + 1) * size, :]


def attend_kernel(
    bk, sub, span, part_ref, pos_ref, q_ref, kv_ref, o_ref, lse_ref, q, keys, values, peak, total, acc, highest
):
    groups, size, bq = q.shape
    tile = pl.program_id(0)

    @pl.when(tile == 0)
    def _():
        for i in range(kv_ref.shape[0]):
            part = slice(i * span, (i + 1) * span)
            keys[part, :] = jnp.transpose(kv_ref[i, :size, :], (1, 0))
            values[:, part] = kv_ref[i, size:, :]

    unpack_blocks(q_ref, q)
    unmasked, ends = key_tiles(tile * bq, bq, sub, span, part_ref[0], bk)

    def reset():
        peak[...] = jnp.full(peak.shape, NEG, F32)
        total[...] = jnp.zeros(total.shape, F32)
        acc[...] = jnp.zeros(acc.shape, F32)

    def part_step(start, rows, cols, masked, moving):
        k = keys[pl.ds(start, rows), :]
        v = values[:, pl.ds(start, rows)]
        if masked:
            shape = (rows, cols.stop - cols.start)
            allowed = (start + lax.broadcasted_iota(jnp.int32, shape, 0)) <= pos_ref[:, cols]

        def score(g):
            scores = jnp.dot(k, q[g, :, cols], preferred_element_type=F32)
            return jnp.where(allowed, scores, NEG) if masked else scores

        ahead = score(0)
        for g in range(groups):
            scores = ahead
            if g + 1 < groups:
                ahead = score(g + 1)
            old = peak[g, :, cols]
            most = jnp.max(scores, axis=0, keepdims=True)
            if moving:
                new = jnp.maximum(old, most)
                factor = jnp.exp2(old - new)
                peak[g, :, cols] = new
                total[g, :, cols] = total[g, :, cols] * factor
                acc[g, :, cols] = acc[g, :, cols] * factor
            else:
                new = old
                highest[g, :, cols] = jnp.maximum(highest[g, :, cols], most)
            weights = jnp.exp2(scores - new)
            total[g, :, cols] += jnp.sum(weights, axis=0, keepdims=True)
            acc[g, :, cols] += jnp.dot(v, weights.astype(BF16), preferred_element_type=F32)

    def step(j, masked, moving):
        for first, rows, cols in tile_parts(bk, bq, sub, span, masked):
            part_step(pl.multiple_of(j * bk + first, rows), rows, cols, masked, moving)

    reset()
    loop(unmasked, ends, lambda j: step(j, True, True))
    highest[...] = peak[...]
    loop(0, unmasked, lambda j: step(j, False, False))

    @pl.when(jnp.max(highest[...] - peak[...]) > 30.0)
    def _():
        reset()
        loop(0, unmasked, lambda j: step(j, False, True))
        loop(unmasked, ends, lambda j: step(j, True, True))

    for g in range(groups):
        out = (acc[g] / total[g]).astype(BF16)
        lse_ref[g] = peak[g] + jnp.log2(total[g])
        for i in range(o_ref.shape[0]):
            o_ref[i, g * size : (g + 1) * size, :] = out[:, i * o_ref.shape[2] : (i + 1) * o_ref.shape[2]]


def attend(part, pos, q, kv, bq, bk, sub, span):
    nq, blocks = pos.shape[1], pos.shape[1] // sub
    nk = blocks * span
    groups, size, rows = GROUP, HEAD_SIZE, QROWS
    tile = pl.BlockSpec((bq // sub, rows, sub), lambda i: (i, 0, 0))
    stat = pl.BlockSpec((groups, 1, bq), lambda i: (0, 0, i))
    return pl.pallas_call(
        functools.partial(attend_kernel, bk, sub, span),
        grid=(nq // bq,),
        in_specs=[
            pl.BlockSpec(memory_space=pltpu.SMEM),
            pl.BlockSpec((1, bq), lambda i: (0, i)),
            tile,
            whole(blocks, 2 * size, span),
        ],
        out_specs=[tile, stat],
        out_shape=[
            jax.ShapeDtypeStruct((blocks, rows, sub), BF16),
            jax.ShapeDtypeStruct((groups, 1, nq), F32),
        ],
        scratch_shapes=[
            pltpu.VMEM((groups, size, bq), BF16),
            pltpu.VMEM((nk, size), BF16),
            pltpu.VMEM((size, nk), BF16),
            pltpu.VMEM((groups, 1, bq), F32),
            pltpu.VMEM((groups, 1, bq), F32),
            pltpu.VMEM((groups, size, bq), F32),
            pltpu.VMEM((groups, 1, bq), F32),
        ],
        compiler_params=params("arbitrary"),
        cost_estimate=COST,
        name="attend",
    )(part, pos, q, kv)


def turn_back(rows, cosine, sine):
    half = HEAD_SIZE // 2
    a, b = rows[:half], rows[half:]
    return jnp.concatenate([a * cosine + b * sine, b * cosine - a * sine], axis=0)


def attend_back_kernel(
    bk, sub, span, part_ref, pos_ref, q_ref, o_ref, do_ref, lse_ref, kv_ref, qtab_ref, ktab_ref, *refs
):
    *outs, q, keys, keys_t, values, q_rows, do, do_rows, delta, dq, dk, dv = refs
    dq_ref, dkv_ref = outs[0], outs[-1]
    groups, size, bq = q.shape
    half = size // 2
    tile = pl.program_id(0)

    @pl.when(tile == 0)
    def _():
        for i in range(kv_ref.shape[0]):
            part = slice(i * span, (i + 1) * span)
            keys[part, :] = jnp.transpose(kv_ref[i, :size, :], (1, 0))
            keys_t[:, part] = kv_ref[i, :size, :]
            values[part, :] = jnp.transpose(kv_ref[i, size:, :], (1, 0))
        dk[...] = jnp.zeros(dk.shape, F32)
        dv[...] = jnp.zeros(dv.shape, F32)

    unpack_blocks(q_ref, q)
    unpack_blocks(do_ref, do)
    pieces, columns = do_ref.shape[0], do_ref.shape[2]
    for g in range(groups):
        for i in range(pieces):
            both = do_ref[i, g * size : (g + 1) * size, :].astype(F32) * o_ref[i, g * size : (g + 1) * size, :].astype(F32)
            delta[g, :, i * columns : (i + 1) * columns] = jnp.sum(both, axis=0, keepdims=True)
        q_rows[g] = jnp.transpose(q[g], (1, 0))
        do_rows[g] = jnp.transpose(do[g], (1, 0))
    dq[...] = jnp.zeros(dq.shape, F32)
    unmasked, ends = key_tiles(tile * bq, bq, sub, span, part_ref[0], bk)

    def step(j, masked):
        start = pl.multiple_of(j * bk, bk)
        k = keys[pl.ds(start, bk), :]
        kt = keys_t[:, pl.ds(start, bk)]
        v = values[pl.ds(start, bk), :]
        if masked:
            allowed = (start + lax.broadcasted_iota(jnp.int32, (bk, bq), 0)) <= pos_ref[...]
        dv_part = jnp.zeros((bk, size), F32)
        dk_part = jnp.zeros((bk, size), F32)
        for g in range(groups):
            scores = jnp.dot(k, q[g], preferred_element_type=F32)
            prob = jnp.exp2(scores - lse_ref[g])
            if masked:
                prob = jnp.where(allowed, prob, 0.0)
            dv_part = dv_part + jnp.dot(prob.astype(BF16), do_rows[g], preferred_element_type=F32)
            dots = jnp.dot(v, do[g], preferred_element_type=F32)
            score_grad = (prob * (dots - delta[g])).astype(BF16)
            dk_part = dk_part + jnp.dot(score_grad, q_rows[g], preferred_element_type=F32)
            dq[g] += jnp.dot(kt, score_grad, preferred_element_type=F32)
        dv[pl.ds(start, bk), :] += dv_part
        dk[pl.ds(start, bk), :] += dk_part

    loop(0, unmasked, lambda j: step(j, False))
    loop(unmasked, ends, lambda j: step(j, True))
    scale = HEAD_SIZE**-0.5
    packed = len(outs) == 1
    for i in range(pieces):
        cols = slice(i * columns, (i + 1) * columns)
        for g in range(groups):
            out = turn_back(dq[g, :, cols], qtab_ref[i, :half], qtab_ref[i, half:])
            dq_ref[tile if packed else i, g * size : (g + 1) * size, :] = (out * scale).astype(BF16)

    @pl.when(tile == pl.num_programs(0) - 1)
    def _():
        base = QROWS if packed else 0
        for i in range(dkv_ref.shape[0]):
            part = slice(i * span, (i + 1) * span)
            back = turn_back(jnp.transpose(dk[part, :], (1, 0)), ktab_ref[i, :half], ktab_ref[i, half:])
            dkv_ref[i, base : base + size, :] = (back * (1.0 / LOG2_E)).astype(BF16)
            dkv_ref[i, base + size : base + 2 * size, :] = jnp.transpose(dv[part, :], (1, 0)).astype(BF16)


def attend_back(part, pos, q, o, do, lse, kv, qtab, ktab, bq, bk, sub, span):
    nq, blocks = pos.shape[1], pos.shape[1] // sub
    nk = blocks * span
    groups, size, rows = GROUP, HEAD_SIZE, QROWS
    tile = pl.BlockSpec((bq // sub, rows, sub), lambda i: (i, 0, 0))
    if sub == span == bq:
        out_specs = [whole(blocks, SLICE, span)]
        out_shape = [jax.ShapeDtypeStruct((blocks, SLICE, span), BF16)]
    else:
        out_specs = [tile, whole(blocks, 2 * size, span)]
        out_shape = [
            jax.ShapeDtypeStruct((blocks, rows, sub), BF16),
            jax.ShapeDtypeStruct((blocks, 2 * size, span), BF16),
        ]
    return pl.pallas_call(
        functools.partial(attend_back_kernel, bk, sub, span),
        grid=(nq // bq,),
        in_specs=[
            pl.BlockSpec(memory_space=pltpu.SMEM),
            pl.BlockSpec((1, bq), lambda i: (0, i)),
            tile,
            tile,
            tile,
            pl.BlockSpec((groups, 1, bq), lambda i: (0, 0, i)),
            whole(blocks, 2 * size, span),
            pl.BlockSpec((bq // sub, size, sub), lambda i: (i, 0, 0)),
            whole(blocks, size, span),
        ],
        out_specs=out_specs,
        out_shape=out_shape,
        scratch_shapes=[
            pltpu.VMEM((groups, size, bq), BF16),
            pltpu.VMEM((nk, size), BF16),
            pltpu.VMEM((size, nk), BF16),
            pltpu.VMEM((nk, size), BF16),
            pltpu.VMEM((groups, bq, size), BF16),
            pltpu.VMEM((groups, size, bq), BF16),
            pltpu.VMEM((groups, bq, size), BF16),
            pltpu.VMEM((groups, 1, bq), F32),
            pltpu.VMEM((groups, size, bq), F32),
            pltpu.VMEM((nk, size), F32),
            pltpu.VMEM((nk, size), F32),
        ],
        compiler_params=params("arbitrary"),
        cost_estimate=COST,
        name="attend_back",
    )(part, pos, q, o, do, lse, kv, qtab, ktab)


def chosen_rows(rank, cap):
    return lax.broadcasted_iota(jnp.int32, (cap, rank.shape[1]), 0) == rank


def dispatch_kernel(cap, rank_ref, token_ref, row_ref):
    for e in range(rank_ref.shape[0]):
        one = chosen_rows(rank_ref[e], cap).astype(F32).astype(BF16)
        row_ref[e] = jnp.dot(one, token_ref[...], preferred_element_type=F32).astype(BF16)


def dispatch(rank, tokens, block, cap, wide):
    count = rank.shape[0]
    span, width = tokens.shape
    return pl.pallas_call(
        functools.partial(dispatch_kernel, cap),
        grid=(width // wide,),
        in_specs=[
            pl.BlockSpec((count, 1, span), lambda i: (0, 0, block)),
            pl.BlockSpec((span, wide), lambda i: (0, i)),
        ],
        out_specs=pl.BlockSpec((count, cap, wide), lambda i: (0, 0, i)),
        out_shape=jax.ShapeDtypeStruct((count, cap, width), BF16),
        compiler_params=params("arbitrary"),
        cost_estimate=COST,
        name="dispatch",
    )(rank, tokens)


def experts_kernel(span, cap, offset, blocks, place_ref, rank_ref, prob_ref, *refs):
    x_refs, g_refs = refs[:blocks], refs[blocks : 2 * blocks]
    gu_ref, dn_ref, back_ref, out_ref, mine_ref, theirs_ref, grads = refs[2 * blocks :]
    e = pl.program_id(0)
    x = jnp.concatenate([ref[0] for ref in x_refs], axis=0)
    g = jnp.concatenate([ref[0] for ref in g_refs], axis=0)
    width = x.shape[1]
    ps = []
    for i in range(blocks):
        rows = slice(i * span, (i + 1) * span)
        hit = chosen_rows(rank_ref[0, :, rows], cap)
        ps.append(jnp.sum(jnp.where(hit, prob_ref[0, :, rows], 0.0), axis=1, keepdims=True))
    prob = jnp.concatenate(ps, axis=0)
    mixed = jnp.dot(x, gu_ref[0], preferred_element_type=F32)
    gate, up = mixed[:, :FFE], mixed[:, FFE:]
    logistic = 1.0 / (1.0 + jnp.exp(-gate))
    act = (gate * logistic * up).astype(BF16)
    sent = (prob * g.astype(F32)).astype(BF16)
    act_grad = contract(sent, dn_ref[0], 1, 1)
    mix = jnp.concatenate(
        [act_grad * up * logistic * (1.0 + gate * (1.0 - logistic)), act_grad * gate * logistic], axis=1
    ).astype(BF16)
    out = jnp.dot(act, dn_ref[0], preferred_element_type=F32).astype(BF16).astype(F32)
    route = jnp.sum(g.astype(F32) * out, axis=1, keepdims=True)
    out_ref[0] = (prob * out).astype(BF16)
    back_ref[0, :, :width] = contract(mix, gu_ref[0], 1, 1).astype(BF16)
    high = route.astype(BF16).astype(F32)
    place = lax.broadcasted_iota(jnp.int32, (route.shape[0], EXTRA), 1) - (place_ref[0] + offset + e)
    extra = jnp.where(place == 0, high, jnp.where(place == EXPERTS, route - high, 0.0))
    back_ref[0, :, width:] = extra.astype(BF16)
    grads[:, : 2 * FFE] = contract(x, mix, 0, 0).astype(BF16)
    grads[:, 2 * FFE :] = contract(sent, act, 0, 0).astype(BF16)
    pairs, _, own, _ = mine_ref.shape
    core = place_ref[1]
    for i in range(pairs):
        mine_ref[i, 0] = grads[pl.ds(pl.multiple_of((2 * i + core) * own, own), own), :]
        theirs_ref[i, 0] = grads[pl.ds(pl.multiple_of((2 * i + 1 - core) * own, own), own), :]


def run_experts(place, rank, prob, xs, gs, gateup, down, offset, count, n_ctx, span, cap):
    blocks = len(xs)
    width = gateup.shape[1]
    rows = blocks * cap
    tokens = blocks * span
    own = width // n_ctx
    pairs = n_ctx // 2

    def picked(*shape):
        return pl.BlockSpec((1,) + shape, lambda e: (e + offset, 0, 0))

    def row(wide):
        return pl.BlockSpec((1, rows, wide), lambda e: (e, 0, 0))

    half = pl.BlockSpec((pairs, 1, own, 3 * FFE), lambda e: (0, e, 0, 0))
    half_shape = jax.ShapeDtypeStruct((pairs, count, own, 3 * FFE), BF16)
    return pl.pallas_call(
        functools.partial(experts_kernel, span, cap, offset, blocks),
        grid=(count,),
        in_specs=[pl.BlockSpec(memory_space=pltpu.SMEM), picked(1, tokens), picked(1, tokens)]
        + [picked(cap, width)] * (2 * blocks)
        + [picked(width, 2 * FFE), picked(FFE, width)],
        out_specs=[row(width + EXTRA), row(width), half, half],
        out_shape=[
            jax.ShapeDtypeStruct((count, rows, width + EXTRA), BF16),
            jax.ShapeDtypeStruct((count, rows, width), BF16),
            half_shape,
            half_shape,
        ],
        scratch_shapes=[pltpu.VMEM((width, 3 * FFE), BF16)],
        compiler_params=params("arbitrary"),
        cost_estimate=pl.CostEstimate(
            flops=2 * count * rows * width * 9 * FFE, bytes_accessed=count * rows * width * 8, transcendentals=0
        ),
        name="experts",
    )(place, rank, prob, *xs, *gs, gateup, down)


def add_kernel(left_ref, right_ref, sum_ref):
    sum_ref[...] = (left_ref[...].astype(F32) + right_ref[...].astype(F32)).astype(BF16)


def add(left, right):
    pairs, count, own, wide = left.shape
    block = pl.BlockSpec((1, 1, own, wide), lambda i, e: (i, e, 0, 0))
    return pl.pallas_call(
        add_kernel,
        grid=(pairs, count),
        in_specs=[block, block],
        out_specs=block,
        out_shape=jax.ShapeDtypeStruct(left.shape, BF16),
        compiler_params=params("arbitrary", "arbitrary"),
        cost_estimate=COST,
        name="add",
    )(left, right)


def outer_kernel(rows_ref, grad_ref, side_ref, full_ref):
    owners, _, piece, _ = full_ref.shape
    width = grad_ref.shape[1]
    product = jnp.dot(rows_ref[...], grad_ref[...], preferred_element_type=F32).astype(BF16)
    for i in range(owners):
        part = slice(i * piece, (i + 1) * piece)
        full_ref[i, 0, :, :width] = product[part]
        full_ref[i, 0, :, width:] = side_ref[part, :]


def outer(rows, grad, side, owners, own):
    height, span = rows.shape
    width = grad.shape[1]
    wide = width + side.shape[1]
    return pl.pallas_call(
        outer_kernel,
        grid=(height // own,),
        in_specs=[
            pl.BlockSpec((own, span), lambda c: (c, 0)),
            whole(span, width),
            pl.BlockSpec((own, side.shape[1]), lambda c: (c, 0)),
        ],
        out_specs=pl.BlockSpec((owners, 1, own // owners, wide), lambda c: (0, c, 0, 0)),
        out_shape=jax.ShapeDtypeStruct((owners, height // own, own // owners, wide), BF16),
        compiler_params=params("arbitrary"),
        cost_estimate=COST,
        name="outer",
    )(rows, grad, side)


def gather_parts_kernel(mixed_ref, head_ref, part_ref):
    count, _, wide = mixed_ref.shape
    part_ref[:, :wide] = sum(mixed_ref[c].astype(F32) for c in range(count)).astype(BF16)
    for h in range(KEY_VALUE_HEADS):
        head = head_ref[h]
        part_ref[:, wide + h * QROWS : wide + (h + 1) * QROWS] = head[:, :QROWS]
        base = wide + KEY_VALUE_HEADS * QROWS
        for i in range(2):
            start = base + (i * KEY_VALUE_HEADS + h) * HEAD_SIZE
            part_ref[:, start : start + HEAD_SIZE] = head[:, QROWS + i * HEAD_SIZE : QROWS + (i + 1) * HEAD_SIZE]


def gather_parts(mixed, heads):
    _, piece, wide = mixed.shape
    total = wide + KEY_VALUE_HEADS * SLICE
    return pl.pallas_call(
        gather_parts_kernel,
        grid=(1,),
        in_specs=[whole(*mixed.shape), whole(*heads.shape)],
        out_specs=whole(piece, total),
        out_shape=jax.ShapeDtypeStruct((piece, total), BF16),
        compiler_params=params("arbitrary"),
        cost_estimate=COST,
        name="gather_parts",
    )(mixed, heads)


def finish_kernel(count, me_ref, *refs):
    blocks, (wq, wk, wv, q_ref, k_ref, v_ref, o_ref, side_ref) = refs[:count], refs[count:]
    piece = blocks[0].shape[0]
    width, heads, pair = q_ref.shape[1], k_ref.shape[1], EXPERTS + 1
    for i in range(count):
        rows = pl.ds(pl.multiple_of((me_ref[0] ^ i) * piece, piece), piece)
        block = blocks[i][...].astype(F32)
        o_ref[rows, :] = block[:, :width]
        start = width + EXTRA
        query, key = block[:, start : start + width], block[:, start + width : start + width + heads]
        value = block[:, start + width + heads :]
        q_ref[rows, :], k_ref[rows, :], v_ref[rows, :] = query, key, value
        inner = jnp.sum(wq[rows, :].astype(F32) * query, axis=1, keepdims=True)
        inner += jnp.sum(wk[rows, :].astype(F32) * key, axis=1, keepdims=True)
        inner += jnp.sum(wv[rows, :].astype(F32) * value, axis=1, keepdims=True)
        column = lax.broadcasted_iota(jnp.int32, (piece, EXTRA), 1)
        side_ref[rows, :] = jnp.where(column == pair, inner, block[:, width:start])


def finish(me, blocks, query_weight, key_matrix, value_matrix):
    weights = [query_weight, key_matrix, value_matrix]
    own, width = query_weight.shape
    shapes = [array.shape for array in weights] + [(own, width), (own, EXTRA)]
    return pl.pallas_call(
        functools.partial(finish_kernel, len(blocks)),
        grid=(1,),
        in_specs=[pl.BlockSpec(memory_space=pltpu.SMEM)] + [whole(*array.shape) for array in [*blocks, *weights]],
        out_specs=[whole(*shape) for shape in shapes],
        out_shape=[jax.ShapeDtypeStruct(shape, F32) for shape in shapes],
        compiler_params=params("arbitrary"),
        cost_estimate=COST,
        name="finish",
    )(me.astype(jnp.int32).reshape(1), *blocks, *weights)


def unpack_kernel(sum_ref, *refs):
    gateup_ref, down_ref = refs[-2:]
    gateup_ref[0] = sum_ref[0, :, : 2 * FFE].astype(F32)
    down_ref[0] = sum_ref[0, :, 2 * FFE :].astype(F32)


def unpack(total, offset, experts, held):
    count, own, wide = total.shape
    return pl.pallas_call(
        unpack_kernel,
        grid=(count,),
        in_specs=[pl.BlockSpec((1, own, wide), lambda e: (e, 0, 0))] + [pl.BlockSpec(memory_space=pl.ANY)] * len(held),
        out_specs=[
            pl.BlockSpec((1, own, 2 * FFE), lambda e: (e + offset, 0, 0)),
            pl.BlockSpec((1, own, FFE), lambda e: (e + offset, 0, 0)),
        ],
        out_shape=[
            jax.ShapeDtypeStruct((experts, own, 2 * FFE), F32),
            jax.ShapeDtypeStruct((experts, own, FFE), F32),
        ],
        input_output_aliases={1 + i: i for i in range(len(held))},
        compiler_params=params("arbitrary"),
        cost_estimate=COST,
        name="unpack",
    )(total, *held)


def combine_kernel(cap, n_parts, *refs):
    rank_refs, row_refs, out_ref = refs[:n_parts], refs[n_parts : 2 * n_parts], refs[-1]
    total = None
    for rank_ref, row_ref in zip(rank_refs, row_refs):
        ones, rows = [], []
        for e in range(rank_ref.shape[0]):
            ones.append(chosen_rows(rank_ref[e], cap).astype(F32).astype(BF16))
            rows.append(row_ref[e])
        part = contract(jnp.concatenate(ones, axis=0), jnp.concatenate(rows, axis=0), 0, 0)
        total = part if total is None else total + part
    out_ref[...] = total.astype(BF16)


def combine(ranks, rows, block, span, cap, wide):
    width = rows[0].shape[2]
    count = sum(r.shape[0] for r in ranks)
    return pl.pallas_call(
        functools.partial(combine_kernel, cap, len(ranks)),
        grid=(width // wide,),
        in_specs=[pl.BlockSpec((r.shape[0], 1, span), lambda i: (0, 0, block)) for r in ranks]
        + [pl.BlockSpec((r.shape[0], cap, wide), lambda i: (0, block, i)) for r in rows],
        out_specs=pl.BlockSpec((span, wide), lambda i: (0, i)),
        out_shape=jax.ShapeDtypeStruct((span, width), BF16),
        compiler_params=params("arbitrary"),
        cost_estimate=COST,
        name="combine",
    )(*ranks, *rows)


def swapped(array, axis, mask):
    count = lax.axis_size(axis)
    return lax.ppermute(array, axis, [(i, i ^ mask) for i in range(count)])


def gather_blocks(array, axis):
    count = lax.axis_size(axis)
    if count != 4:
        return [array] + [swapped(array, axis, k) for k in range(1, count)]
    half = array.shape[0] // 2
    one, two = swapped(array, axis, 1), swapped(array, axis, 2)
    far = jnp.concatenate([swapped(two[:half], axis, 1), swapped(one[half:], axis, 2)], axis=0)
    return [array, one, two, far]


def gather_start(array, axis):
    return [array, swapped(array, axis, 1), swapped(array, axis, 2)]


def gather_end(array, one, two, axis):
    count = lax.axis_size(axis)
    if count != 4:
        return [array, one, two] + [swapped(array, axis, k) for k in range(3, count)]
    half = array.shape[0] // 2
    far = jnp.concatenate([swapped(two[:half], axis, 1), swapped(one[half:], axis, 2)], axis=0)
    return [array, one, two, far]


def gather_rows(array, axis, use, early):
    count = lax.axis_size(axis)
    if count != 4:
        return [use(block, k) for k, block in enumerate(gather_blocks(array, axis))], early
    half = array.shape[0] // 2
    one, two = swapped(array, axis, 1), swapped(array, axis, 2)
    own = use(array, 0)
    own, one, two, early = lax.optimization_barrier((own, one, two, early))
    far = jnp.concatenate([swapped(two[:half], axis, 1), swapped(one[half:], axis, 2)], axis=0)
    one, two, far = lax.optimization_barrier((use(one, 1), use(two, 2), far))
    return [own, one, two, use(far, 3)], early


def wide_sum(*arrays):
    return sum(array.astype(F32) for array in arrays)


def return_start(parts, axis):
    if lax.axis_size(axis) != 4:
        return [parts[0]] + [swapped(parts[k], axis, k) for k in range(1, len(parts))]
    own, one, two, far = parts
    half = own.shape[0] // 2
    via_one, via_two = swapped(far[:half], axis, 1), swapped(far[half:], axis, 2)
    return [own, one, two, via_one, via_two, swapped(one[:half], axis, 1), swapped(two[half:], axis, 2)]


def return_end(held, axis):
    if lax.axis_size(axis) != 4:
        return wide_sum(*held)
    own, one, two, via_one, via_two, one_low, two_high = held
    half = own.shape[0] // 2
    one_high = swapped(wide_sum(one[half:], via_two).astype(BF16), axis, 1)
    two_low = swapped(wide_sum(two[:half], via_one).astype(BF16), axis, 2)
    return jnp.concatenate(
        [wide_sum(own[:half], one_low, two_low), wide_sum(own[half:], one_high, two_high)], axis=0
    )


def for_partners(array, axis, dim):
    count, me = lax.axis_size(axis), lax.axis_index(axis)
    return [lax.dynamic_index_in_dim(array, me ^ k, dim, keepdims=False) for k in range(count)]


def sum_from_partners(parts, axis):
    return wide_sum(parts[0], *[swapped(parts[k], axis, k) for k in range(1, len(parts))]).astype(BF16)


def in_order(blocks, axis):
    me = lax.axis_index(axis)
    blocks = jnp.stack(blocks)
    return jnp.stack([lax.dynamic_index_in_dim(blocks, me ^ k, 0, keepdims=False) for k in range(blocks.shape[0])])


def all_of_expert(array):
    count = lax.axis_size("expert")
    return in_order([array] + [swapped(array, "expert", k) for k in range(1, count)], "expert")


def norm_rows(values, gain):
    factor = lax.rsqrt(jnp.mean(values * values, axis=-1, keepdims=True) + EPS)
    return (values * factor * gain).astype(BF16), factor


def norm_back(grad_norm, values, factor, gain):
    inner = grad_norm * gain
    return factor * inner - values * factor**3 * jnp.mean(inner * values, axis=-1, keepdims=True)


def angles(positions):
    half = HEAD_SIZE // 2
    freq = jnp.power(THETA, -jnp.arange(half).astype(F32) / half)
    turned = freq[None, :, None] * positions.astype(F32)[:, None, :]
    return jnp.concatenate([jnp.cos(turned), jnp.sin(turned)], axis=1)


def per_device(
    inputs,
    cotangent,
    routes,
    attn_gain,
    query_weight,
    key_matrix,
    value_matrix,
    output_matrix,
    ffn_gain,
    router_weight,
    gateup_weight,
    down_weight,
):
    _, span, width = inputs.shape
    n_ctx = lax.axis_size("ctx")
    n_owner = lax.axis_size("expert")
    own_rows = query_weight.shape[0]
    local_experts = gateup_weight.shape[0]
    cap = span // 4
    parts = n_ctx // KEY_VALUE_HEADS
    sub = span // parts
    part = lax.axis_index("ctx") % parts
    part_arg = part.astype(jnp.int32).reshape(1)

    tokens_in = inputs.reshape(span, width)
    me = lax.axis_index("expert")
    piece = own_rows // n_owner

    def a_part(array):
        return lax.dynamic_slice_in_dim(array, me * piece, piece, 0)

    heads = jnp.concatenate(
        [
            a_part(query_weight).reshape(piece, KEY_VALUE_HEADS, QROWS),
            a_part(key_matrix).reshape(piece, KEY_VALUE_HEADS, HEAD_SIZE),
            a_part(value_matrix).reshape(piece, KEY_VALUE_HEADS, HEAD_SIZE),
        ],
        axis=-1,
    ).transpose(1, 0, 2)
    small = jnp.concatenate([attn_gain[:, None], ffn_gain[:, None], router_weight], axis=1)
    small = a_part(jnp.pad(small, ((0, 0), (0, HEAD_SIZE - small.shape[1]))))
    sends = jnp.concatenate(
        [jnp.repeat(heads, parts, axis=0), jnp.broadcast_to(small[None], (n_ctx,) + small.shape)], axis=-1
    )
    weights = all_of_expert(lax.all_to_all(sends, "ctx", 0, 0, tiled=True))
    weights = weights.transpose(1, 0, 2, 3).reshape(width, -1)
    head_weight = weights[:, :SLICE].T
    gain_one = weights[:, SLICE].astype(F32)
    gain_two = weights[:, SLICE + 1].astype(F32)
    router = weights[:, SLICE + 2 : SLICE + 2 + EXPERTS]

    names = routes.reshape(span, TOPK)
    hits = jnp.any(names[:, :, None] == jnp.arange(EXPERTS), axis=1)
    upto = (jnp.arange(span)[:, None] <= jnp.arange(span)[None, :]).astype(BF16)
    counted = contract(hits.astype(BF16), upto, 0, 0)
    ranks = jnp.where(hits.T, counted - 1.0, -1.0).astype(BF16)

    def to_owners(array):
        array = lax.all_to_all(array.reshape(n_owner, local_experts, span), "expert", 0, 0, tiled=True)
        blocks = [lax.dynamic_index_in_dim(array, me ^ k, 0, keepdims=False) for k in range(n_owner)]
        return jnp.concatenate(blocks, axis=1)[:, None]

    every = jnp.arange(n_ctx * span, dtype=jnp.int32).reshape(n_ctx, span)
    table = angles(every)
    cut = span * 3 // 4 if span % 512 == 0 else span // 2
    x_pieces = [
        lax.all_gather(part_in, "ctx", axis=0, tiled=False) for part_in in (tokens_in[:cut], tokens_in[cut:])
    ]
    grad_in = cotangent.reshape(span, width)
    held = gather_start(grad_in, "expert")
    rank = to_owners(ranks)
    x_pieces[0], held, head_weight, rank = lax.optimization_barrier((x_pieces[0], held, head_weight, rank))
    rank = rank.astype(jnp.int32)
    grad_blocks = gather_end(*held, "expert")
    buffers = project(x_pieces[0], gain_one[None], head_weight, table, 0, ())
    x_pieces[1], grad_blocks, buffers = lax.optimization_barrier((x_pieces[1], grad_blocks, buffers))
    normed_all, q_all, kv_all = project(x_pieces[1], gain_one[None], head_weight, table, cut // (span - cut), buffers)
    if parts == 1:
        queries, positions, q_table = q_all, every, table
    else:

        def mine(array):
            array = array.reshape(array.shape[:-1] + (parts, sub))
            return lax.dynamic_index_in_dim(array, part, array.ndim - 2, keepdims=False)

        queries, positions, q_table = mine(q_all), mine(every), mine(table)
    pos = positions.reshape(1, -1)

    output_matrix, w_heads, queries = lax.optimization_barrier((output_matrix, head_weight, queries))
    w_output = lax.all_gather(output_matrix, "ctx", axis=0, tiled=True)
    grad_rows = [dispatch(rank, block, k, cap, width // 2) for k, block in enumerate(grad_blocks)]
    tile = min(512, n_ctx * sub)
    attended, lse = attend(part_arg, pos, queries, kv_all, tile, tile, sub, span)

    def to_rows(array):
        array = lax.all_to_all(array, "ctx", 0, 0, tiled=True)
        array = array.reshape(KEY_VALUE_HEADS, parts, -1, sub).transpose(0, 2, 1, 3)
        return array.reshape(-1, span)

    attended_rows, grad_rows = lax.optimization_barrier((to_rows(attended), grad_rows))
    flat_in = tokens_in.astype(F32)
    hidden = flat_in + contract(attended_rows, w_output, 0, 0)
    normed_two, rms_two = norm_rows(hidden, gain_two)
    w_heads, normed_two = lax.optimization_barrier((w_heads, normed_two))
    w_heads = lax.all_gather(w_heads, "ctx", axis=0, tiled=False)[::parts].reshape(-1, width)
    logits = jnp.dot(normed_two, router, preferred_element_type=F32)
    masked = jnp.where(hits, logits, NEG)
    powers = jnp.where(hits, jnp.exp(masked - jnp.max(masked, axis=-1, keepdims=True)), 0.0)
    probs = powers / jnp.sum(powers, axis=-1, keepdims=True)
    prob = to_owners(probs.T)

    place = jnp.stack([me * local_experts, lax.axis_index("ctx") % 2]).astype(jnp.int32)
    token_rows, prob = gather_rows(
        normed_two, "expert", lambda block, k: dispatch(rank, block, k, cap, width // 2), prob
    )
    cuts, offset = [], 0
    for count in (1, 1, 3, 3, local_experts):
        if offset < local_experts:
            cuts.append((offset, min(count, local_experts - offset)))
            offset += count
    backs, outs, sums = [], [], []
    core_line = [[z * 2 + core for z in range(n_ctx // 2)] for core in range(2)]

    def line_sum(pair):
        total = lax.psum_scatter(
            pair.reshape(-1, 3 * FFE), "ctx", scatter_dimension=0, tiled=True, axis_index_groups=core_line
        )
        return total.reshape(-1, own_rows, 3 * FFE)

    pairs, pair_sums = [], []
    for number, (offset, count) in enumerate(cuts):
        if number == 1:
            w_heads, place, _ = lax.optimization_barrier((w_heads, place, backs[0]))
        elif number > 1:
            if number > 2:
                pairs[number - 2], _ = lax.optimization_barrier((pairs[number - 2], backs[-1]))
            pair_sums.append(add(*pairs[number - 2]))
            place, _, _ = lax.optimization_barrier((place, backs[-1], pair_sums[-1]))
        back, out, mine, theirs = run_experts(
            place, rank, prob, token_rows, grad_rows, gateup_weight, down_weight, offset, count, n_ctx, span, cap
        )
        backs.append(back)
        outs.append(out)
        pairs.append((mine, swapped(theirs, "ctx", 1)))
        if number > 1:
            sums.append(line_sum(pair_sums[-1]))
    ranks = [rank[offset : offset + count] for offset, count in cuts]

    def to_tokens(rows):
        return [combine(ranks, rows, k, span, cap, rows[0].shape[2]) for k in reversed(range(n_owner))][::-1]

    back_sum = return_end(return_start(to_tokens(backs), "expert"), "expert")

    grad = cotangent.reshape(span, width).astype(F32)
    route_grad = back_sum[:, width : width + EXPERTS] + back_sum[:, width + EXPERTS : width + 2 * EXPERTS]
    chosen_grad = probs * (route_grad - jnp.sum(probs * route_grad, axis=-1, keepdims=True))
    logit_grad = chosen_grad.astype(BF16)
    normed_two_grad = back_sum[:, :width] + contract(logit_grad, router, 1, 1)
    ffn_gain_full = jnp.sum(normed_two_grad * hidden * rms_two, axis=0)
    hidden_grad = grad + norm_back(normed_two_grad, hidden, rms_two, gain_two)
    hidden_low = hidden_grad.astype(BF16)
    attended_grad = contract(w_output, hidden_low, 1, 1).astype(BF16)
    attended_grad, hidden_low, logit_grad, pairs = lax.optimization_barrier(
        (attended_grad, hidden_low, logit_grad, pairs[-2:])
    )
    sums.append(line_sum(add(*pairs[0])))
    router_full = contract(normed_two, logit_grad, 0, 0)
    attended_grad = attended_grad.reshape(KEY_VALUE_HEADS, QROWS, parts, sub).transpose(0, 2, 1, 3)
    attended_grad = lax.all_to_all(attended_grad.reshape(n_ctx, QROWS, sub), "ctx", 0, 0, tiled=True)
    column = jnp.arange(EXTRA)[None]
    side = jnp.where(
        column == EXPERTS, ffn_gain_full[:, None], jnp.pad(router_full, ((0, 0), (0, EXTRA - EXPERTS)))
    ).astype(BF16)
    mixed_parts = for_partners(outer(attended_rows, hidden_low, side, n_owner, own_rows), "expert", 0)
    earlier = sums[:-1]
    pairs[1], outs, earlier, mixed_parts = lax.optimization_barrier((pairs[1], outs, earlier, mixed_parts))
    pair = add(*pairs[1])
    grads = ()
    for (offset, _), total in zip(cuts, earlier):
        grads = unpack(total, offset, local_experts, grads)
    out_parts, attended_grad, grads, mixed_part, pair = lax.optimization_barrier(
        (to_tokens(outs), attended_grad, grads, sum_from_partners(mixed_parts, "expert"), pair)
    )
    mixed_part = lax.all_to_all(mixed_part, "ctx", 0, 0, tiled=True)
    backs = attend_back(
        part_arg, pos, queries, attended, attended_grad, lse, kv_all, q_table, table, tile, tile, sub, span
    )
    mixed_part, backs = lax.optimization_barrier((mixed_part, backs))
    if len(backs) == 1:
        rows_back = lax.all_to_all(backs[0], "ctx", 0, 0, tiled=True).reshape(-1, span)
        head_grad = head_grads(backs[0], normed_all)
    else:
        query_back, kv_back = backs
        query_rows = to_rows(query_back).reshape(KEY_VALUE_HEADS, QROWS, span)
        kv_rows = lax.all_to_all(kv_back, "ctx", 0, 0, tiled=True).astype(F32)
        kv_rows = jnp.sum(kv_rows.reshape(KEY_VALUE_HEADS, parts, 2 * HEAD_SIZE, span), axis=1).astype(BF16)
        rows_back = jnp.concatenate([query_rows, kv_rows], axis=1).reshape(-1, span)
        normed_part = normed_all.reshape(n_ctx, parts, sub, width)
        normed_part = lax.dynamic_index_in_dim(normed_part, part, 1, keepdims=False)
        head_grad = jnp.concatenate([head_grads(query_back, normed_part), head_grads(kv_back, normed_all)], axis=1)
    head_parts = for_partners(head_grad.reshape(n_ctx, n_owner, -1, SLICE), "expert", 1)
    head_part = sum_from_partners(head_parts, "expert")
    grads = unpack(sums[-1], cuts[-2][0], local_experts, grads)
    pair, rows_back, head_part = lax.optimization_barrier((pair, rows_back, head_part))
    head_part, out_parts = lax.optimization_barrier((head_part, out_parts))
    head_part = lax.all_to_all(head_part, "ctx", 0, 0, tiled=True)
    output = hidden + return_end(return_start(out_parts, "expert"), "expert")
    output = output.astype(BF16).reshape(1, span, width)
    sums.append(line_sum(pair))
    gateup_grad, down_grad = unpack(sums[-1], cuts[-1][0], local_experts, grads)
    down_grad = down_grad.transpose(0, 2, 1)
    if parts > 1:
        head_part = jnp.sum(head_part.astype(F32).reshape(KEY_VALUE_HEADS, parts, piece, SLICE), axis=1).astype(BF16)
    summed = gather_parts(mixed_part, head_part)
    summed = [summed] + [swapped(summed, "expert", k) for k in range(1, n_owner)]
    place = me
    if piece % 16:
        summed, place = [in_order(summed, "expert").reshape(own_rows, -1)], 0 * me
    query_grad, key_grad, value_grad, outproj_grad, side = finish(
        place, summed, query_weight, key_matrix, value_matrix
    )
    router_grad, ffn_gain_grad = side[:, :EXPERTS], side[:, EXPERTS]
    attn_gain_grad = side[:, EXPERTS + 1] / attn_gain.astype(F32)
    normed_one_grad = contract(rows_back, w_heads, 0, 0)
    rms_one = lax.rsqrt(jnp.mean(flat_in * flat_in, axis=-1, keepdims=True) + EPS)
    input_grad = (
        (hidden_grad + norm_back(normed_one_grad, flat_in, rms_one, gain_one)).astype(BF16).reshape(1, span, width)
    )
    return (
        output,
        input_grad,
        attn_gain_grad,
        query_grad,
        key_grad,
        value_grad,
        outproj_grad,
        ffn_gain_grad,
        router_grad,
        gateup_grad,
        down_grad,
    )


def solution(mesh):
    tokens = P("expert", "ctx", None)
    row = P("ctx")
    rows = P("ctx", None)
    owned = P("expert", None, None)
    return jax.shard_map(
        per_device,
        mesh=mesh,
        in_specs=(tokens, tokens, tokens, row, rows, rows, rows, rows, row, rows, owned, owned),
        out_specs=(
            tokens,
            tokens,
            row,
            rows,
            rows,
            rows,
            rows,
            row,
            rows,
            P("expert", "ctx", None),
            P("expert", None, "ctx"),
        ),
        check_vma=False,
    )
```
